512 devices in a mesh: gx: 64 (over y, x, core), gy: 8 (over z).
Axes of the slice: x: 4, y: 8, z: 8, core: 2. Of those that a mesh axis runs over, the one named last changes fastest.
Arguments:
- residual: float32 [64, 256, 2048], P(None, 'gx', 'gy'), may hold values from -6 to 6
- classes: int32 [64, 256, 2048], P(None, 'gx', 'gy'), may hold values from 0 to 15
- class_perm: float32 [16], replicated, may hold values from 0.1 to 10
- support: int32 [64, 256, 2048], P(None, 'gx', 'gy'), may hold values from 0 to 15
- coarse_inverse: float32 [8192, 8192], P(('gx', 'gy')), may hold values from -0.00020716019 to 0.0071875
Outputs:
- preconditioned: float32 [64, 256, 2048], P(None, 'gx', 'gy')
The draws below stay inside these ranges and needn't reach their ends.
All inputs are finite; a program needn't handle non-finite values.
Results may differ from the reference program's by a relative error of at most 0.0003.
Values sent between devices are 32-bit elements; how exact they have to be, the bound alone decides.
No kernel may reach another device: no remote copies, remote signals or barrier semaphores. Data moves between devices by JAX's collectives and lax.ppermute only.
A program may use at most 64 MiB of HBM per device.

```python
import math
import jax
import jax.numpy as jnp
from jax import lax

CX = 4
CY = 256
NZ = 64
CF = 16
NCLASS = 16
SWEEPS = 4
NX = 256
NY = 2048
NC = 8192
AGG = 4096
N_GY = 8


def draw_support(key, part):
    key = jax.random.fold_in(key, 5)
    first, second = jax.random.split(key)
    half_count = CF // 2
    x_local = jnp.arange(NX) % CX
    y_local = jnp.arange(NY) % CY
    block_id = (x_local * 2 // CX)[:, None] * half_count + (y_local * half_count // CY)[None, :]
    block_id = jnp.broadcast_to(block_id[None, :, :], (NZ, NX, NY))
    replace_mask = jax.random.randint(first, (NZ, NX, NY), 0, 4) == 0
    scattered = jax.random.randint(second, (NZ, NX, NY), 0, CF)
    return jnp.where(replace_mask, scattered, block_id).astype(jnp.int32)


def draw_coarse_inverse(key, part):
    key = jax.random.fold_in(key, 11)
    first, second = jax.random.split(key)
    off_scale = 0.3 * (AGG * NC) ** (-0.5)
    outside = jnp.clip(jax.random.normal(first, (NC, NC), jnp.float32), -4.0, 4.0) * off_scale
    leading = jax.random.uniform(second, (NC,), jnp.float32, 0.5, 1.5) * 0.3 * AGG ** (-0.5)
    rows = jnp.arange(NC)
    on_diag = rows[:, None] == rows[None, :]
    return jnp.where(on_diag, leading[:, None], outside).astype(jnp.float32)


def touch_ends(values, rng, least, top_value):
    extent = values.shape
    place = [jax.random.randint(jax.random.fold_in(rng, axis), (), 0, extent[axis]) for axis in range(len(extent))]
    values = values.at[tuple(place)].set(least)
    longest = extent.index(max(extent))
    place[longest] = (place[longest] + 1) % extent[longest]
    return values.at[tuple(place)].set(top_value)


def levels(rng, shape, cuts, smallest, high):
    gain = 1.0
    for position, blocks in cuts:
        heights = jax.random.uniform(jax.random.fold_in(jax.random.fold_in(rng, 6), position), (blocks,), jnp.float32, smallest / len(cuts), high / len(cuts))
        gain = gain * jnp.repeat(jnp.exp(heights), shape[position] // blocks).reshape((-1,) + (1,) * (len(shape) - 1 - position))
    return gain


def gaussian(stream_key, dims, deviation, bound, pieces=(), held_as=jnp.bfloat16):
    result = deviation * jax.random.normal(stream_key, dims, jnp.float32)
    if pieces:
        result = result * levels(stream_key, dims, pieces, -0.22, 0.18)
    return jnp.clip(result, -bound, bound).astype(held_as)


def setup_inputs(seed: int = 0) -> dict:
    keys = jax.random.split(jax.random.key(seed), 6)
    return {
        "residual": gaussian(keys[0], (NZ, NX, NY), 1.0, 6.0, ((1, 64), (2, 8)), jnp.float32),
        "classes": touch_ends(jax.random.randint(keys[1], (NZ, NX, NY), 0, NCLASS), jax.random.fold_in(keys[1], 1), 0, NCLASS - 1).astype(jnp.int32),
        "class_perm": jnp.clip(jnp.exp(jax.random.uniform(keys[2], (NCLASS,), jnp.float32, math.log(0.1), math.log(10.0))), 0.1, 10.0),
        "support": draw_support(jax.random.fold_in(keys[5], 71), 0),
        "coarse_inverse": draw_coarse_inverse(jax.random.fold_in(keys[5], 71), 0),
    }


lower_bound = 0.1
upper_bound = 2.0


def neighbours():
    return [(0, -1), (0, 1), (1, -1), (1, 1), (2, -1), (2, 1)]


def shifted(padded, along, offset):
    window = [slice(1, -1), slice(1, -1), slice(1, -1)]
    window[along] = slice(1 + offset, padded.shape[along] - 1 + offset)
    return padded[tuple(window)]


def couplings(perm_pad, inside_pad):
    center = shifted(perm_pad, 0, 0)
    links = []
    for along, offset in neighbours():
        beside = shifted(perm_pad, along, offset)
        beside_in = shifted(inside_pad, along, offset) > 0
        harmonic = 2.0 * center * beside / (center + jnp.where(beside_in, beside, 1.0))
        links.append(jnp.where(beside_in, harmonic, 2.0 * center))
    return links


def operate(padded, links, diagonal):
    summed = diagonal * shifted(padded, 0, 0)
    for link, pair in zip(links, neighbours()):
        summed = summed - link * shifted(padded, pair[0], pair[1])
    return summed


def chebyshev(source, links, diagonal, extend):
    middle = 0.5 * (upper_bound + lower_bound)
    spread = 0.5 * (upper_bound - lower_bound)
    sigma_ratio = middle / spread
    weight_old = 1.0 / sigma_ratio
    inverse_diag = 1.0 / diagonal
    update = inverse_diag * source / middle
    smooth = update
    remain = source
    for sweep in range(SWEEPS - 1):
        remain = remain - operate(extend(update), links, diagonal)
        weight_new = 1.0 / (2.0 * sigma_ratio - weight_old)
        update = weight_new * weight_old * update + (2.0 * weight_new / spread) * inverse_diag * remain
        smooth = smooth + update
        weight_old = weight_new
    return smooth


def pad_all(field):
    return jnp.pad(field, 1)


def reference(residual, classes, class_perm, support, coarse_inverse):
    perm = jnp.take(class_perm, classes)
    perm_pad = jnp.pad(perm, 1)
    inside_pad = jnp.pad(jnp.ones_like(perm), 1)
    links = couplings(perm_pad, inside_pad)
    diagonal = links[0]
    for link in links[1:]:
        diagonal = diagonal + link
    smooth = chebyshev(residual, links, diagonal, pad_all)
    x_device = jnp.arange(NX) // CX
    y_device = jnp.arange(NY) // CY
    device_id = x_device[:, None] * N_GY + y_device[None, :]
    global_id = (device_id[None, :, :] * CF + support).astype(jnp.int32)
    coarse_rhs = jax.ops.segment_sum(residual.reshape(-1), global_id.reshape(-1), num_segments=NC)
    coarse_values = jnp.dot(coarse_inverse, coarse_rhs, precision=lax.Precision.HIGHEST)
    correction = jnp.take(coarse_values, global_id)
    return smooth + correction
```

```python
import functools

import jax
import jax.numpy as jnp
from jax import lax
from jax.experimental import pallas as pl
from jax.experimental.pallas import tpu as pltpu
from jax.sharding import PartitionSpec as P

SWEEPS = 4
LOWER, UPPER = 0.1, 2.0
CF = 16
NZ, CX, LANES = 64, 4, 128
TILES = 2
ROWS = NZ * CX * TILES
STEP = CX * TILES
DEPTH = 4
WIDE = CX + 2 * DEPTH


def iota(shape, dim):
    return lax.broadcasted_iota(jnp.int32, shape, dim)


def inverse(value):
    guess = pl.reciprocal(value, approx=True)
    return guess * (2.0 - value * guess)


def rows_of(block):
    split = block.reshape(NZ, CX, TILES, LANES)
    return split.transpose(0, 2, 1, 3).reshape(ROWS, LANES)


def block_of(rows):
    split = rows.reshape(NZ, TILES, CX, LANES)
    return split.transpose(0, 2, 1, 3).reshape(NZ, CX, TILES * LANES)


def lane_table(entry, count):
    lane = iota((8, LANES), 1)
    table = jnp.zeros((8, LANES), jnp.float32)
    for c in range(count):
        table = jnp.where(lane == c, entry(c), table)
    return table


def pick(table, index):
    return jnp.take_along_axis(table, index, axis=1, mode="promise_in_bounds")


def column_to_lanes(column, first):
    place = iota((CF, LANES), 1) == iota((CF, LANES), 0) + first
    return jnp.sum(jnp.where(place, column, 0.0), axis=0, keepdims=True)


def coarse_kernel(residual_ref, support_ref, message_ref):
    def step(i, sums):
        at = pl.ds(pl.multiple_of(i * 8, 8), 8)
        value, which = residual_ref[at, :], support_ref[at, :]
        return tuple(s + jnp.where(which == c, value, 0.0) for c, s in enumerate(sums))

    zero = jnp.zeros((8, LANES), jnp.float32)
    sums = lax.fori_loop(0, ROWS // 8, step, (zero,) * CF, unroll=4)
    rows = jnp.concatenate([jnp.sum(s, axis=0, keepdims=True) for s in sums], axis=0)
    column = jnp.sum(rows, axis=1, keepdims=True)
    row = column_to_lanes(column, lax.axis_index("gy") * CF)
    message_ref[...] = jnp.broadcast_to(row[None], message_ref.shape)


def pack_kernel(perm_ref, residual_ref, classes_ref, payload_ref, edge_ref):
    table = lane_table(lambda c: 1.0 / jnp.full((8, LANES), perm_ref[c]), perm_ref.shape[0])

    def step(i, carry):
        at = pl.ds(pl.multiple_of(i * 8, 8), 8)
        payload_ref[at, :] = pick(table, classes_ref[at, :])
        payload_ref[pl.ds(pl.multiple_of(ROWS + i * 8, 8), 8), :] = residual_ref[at, :]
        return carry

    lax.fori_loop(0, ROWS // 8, step, 0, unroll=8)
    lane = iota((NZ, LANES), 1)
    edge = jnp.zeros((NZ, LANES), jnp.float32)
    for item in range(2 * CX):
        first = (item // CX) * ROWS + item % CX
        low = payload_ref[pl.ds(first, NZ, stride=STEP), :]
        high = payload_ref[pl.ds(first + CX, NZ, stride=STEP), :]
        both = jnp.where(lane < 64, low, high)
        if item:
            both = pltpu.roll(both, 8 * item, 1)
        edge = jnp.where((lane + 4) % LANES // 8 == item, both, edge)
    edge_ref[...] = edge


def merge_kernel(payload_ref, above_ref, below_ref, out_ref, sem):
    copy = pltpu.make_async_copy(payload_ref, out_ref.at[pl.ds(0, 2 * ROWS), :], sem)
    copy.start()
    lane = iota((NZ, LANES), 1)
    out_ref[pl.ds(2 * ROWS, NZ), :] = jnp.where(lane % 8 < 4, above_ref[...], below_ref[...])
    copy.wait()


def smooth_kernel(low_ref, own_ref, high_ref, out_ref, res, upd, rem, inv, tx, ty, tz, tzb, flux, total):
    middle = 0.5 * (UPPER + LOWER)
    spread = 0.5 * (UPPER - LOWER)
    sigma = middle / spread
    lane = iota((NZ, LANES), 1)
    row = iota((NZ, LANES), 0)
    halo = (lane < 4) | (lane >= LANES - 4)

    for part, ref in enumerate((low_ref, own_ref, high_ref)):
        edge = ref[pl.ds(2 * ROWS, NZ), :]
        for x in range(CX):
            i = part * CX + x
            for t in range(TILES):
                res[i, t] = ref[pl.ds(t * CX + x, NZ, stride=STEP), :]
                rem[i, t] = ref[pl.ds(ROWS + t * CX + x, NZ, stride=STEP), :]
            for item, plane in ((x, res), (CX + x, rem)):
                moved = pltpu.roll(edge, (LANES - 8 * item) % LANES, 1) if item else edge
                plane[i, TILES] = jnp.where(halo, moved, 0.0)

    def link(a, b):
        return 2.0 * inverse(jnp.maximum(a + b, 1e-3))

    def right(values):
        rolled = [pltpu.roll(v, LANES - 1, 1) for v in values]
        n = len(values)
        return [jnp.where(lane == LANES - 1, rolled[(t + 1) % n], rolled[t]) for t in range(n)]

    def left(values, count):
        rolled = [pltpu.roll(v, 1, 1) for v in values]
        return [jnp.where(lane == 0, rolled[t - 1], rolled[t]) for t in range(count)]

    def down(value):
        return jnp.where(row == NZ - 1, 0.0, pltpu.roll(value, NZ - 1, 0))

    def up(value, first):
        rolled = pltpu.roll(value, 1, 0)
        top = jnp.where(row[:8] == 0, first, rolled[:8])
        return jnp.concatenate([top, rolled[8:]], axis=0)

    tiles = range(TILES + 1)
    for t in tiles:
        tx[0, t] = link(res[0, t], res[1, t])

    def setup(i, carry):
        r = [res[i, t] for t in tiles]
        r_right = right(r)
        ly = [link(r[t], r_right[t]) for t in tiles]
        ly_left = left(ly, TILES + 1)
        for t in tiles:
            lx = link(r[t], res[i + 1, t])
            lz = link(r[t], down(r[t]))
            first = link(r[t][:8], 0.0)
            diagonal = lx + tx[i - 1, t] + ly[t] + ly_left[t] + lz + up(lz, first)
            inv_diag = jnp.where(r[t] > 0.0, inverse(diagonal), 0.0)
            tx[i, t], ty[i, t], tz[i, t], tzb[i, t] = lx, ly[t], lz, first
            inv[i, t] = inv_diag
            update = inv_diag * rem[i, t] * (1.0 / middle)
            upd[i, t] = update
            if t < TILES:
                total[i, t] = update
        return carry

    lax.fori_loop(1, WIDE - 1, setup, 0)

    weight_old = 1.0 / sigma
    for sweep in range(1, SWEEPS):
        last = sweep == SWEEPS - 1
        begin, end = 1 + sweep, WIDE - 1 - sweep
        weight_new = 1.0 / (2.0 * sigma - weight_old)
        keep, gain = weight_new * weight_old, 2.0 * weight_new / spread
        weight_old = weight_new
        done = range(TILES) if last else tiles
        for t in done:
            flux[t] = tx[begin - 1, t] * (upd[begin - 1, t] - upd[begin, t])

        def step(i, carry):
            u = [upd[i, t] for t in tiles]
            u_right = right(u)
            fy = [ty[i, t] * (u[t] - u_right[t]) for t in tiles]
            fy_left = left(fy, len(done))
            for t in done:
                fx = tx[i, t] * (u[t] - upd[i + 1, t])
                fz = tz[i, t] * (u[t] - down(u[t]))
                applied = fx - flux[t] + (fy[t] - fy_left[t]) + (fz - up(fz, -tzb[i, t] * u[t][:8]))
                flux[t] = fx
                remain = rem[i, t] - applied
                new = keep * u[t] + gain * inv[i, t] * remain
                if last:
                    out_ref[pl.ds(t * CX + i - DEPTH, NZ, stride=STEP), :] = total[i, t] + new
                else:
                    rem[i, t] = remain
                    upd[i, t] = new
                    if t < TILES:
                        total[i, t] = total[i, t] + new
            return carry

        lax.fori_loop(begin, end, step, 0)


def correct_kernel(gathered_ref, inverse_ref, support_ref, smooth_ref, out_ref):
    zero = jnp.zeros((CF, LANES), jnp.float32)
    sums = [zero] * 4
    count = gathered_ref.shape[0]
    for q in range(count):
        part = inverse_ref[:, q * LANES : (q + 1) * LANES] * gathered_ref[pl.ds(q, 1), :]
        sums[q % 4] = sums[q % 4] + part
    column = jnp.sum((sums[0] + sums[1]) + (sums[2] + sums[3]), axis=1, keepdims=True)
    table = jnp.broadcast_to(column_to_lanes(column, 0), (8, LANES))

    def step(i, carry):
        at = pl.ds(pl.multiple_of(i * 8, 8), 8)
        out_ref[at, :] = smooth_ref[at, :] + pick(table, support_ref[at, :])
        return carry

    lax.fori_loop(0, ROWS // 8, step, 0, unroll=8)


def vmem(count):
    return [pl.BlockSpec(memory_space=pltpu.VMEM)] * count


def call(kernel, outs, ins, args, scratch=(), flops=0, name=None):
    size = sum(a.size * 4 for a in args) + sum(o.size * 4 for o in outs)
    return pl.pallas_call(
        kernel,
        out_shape=outs,
        in_specs=ins,
        out_specs=vmem(len(outs)),
        scratch_shapes=scratch,
        compiler_params=pltpu.CompilerParams(vmem_limit_bytes=24 * 1024 * 1024),
        cost_estimate=pl.CostEstimate(flops=flops, bytes_accessed=size, transcendentals=0),
        name=name,
    )(*args)


def floats(*shape):
    return jax.ShapeDtypeStruct(shape, jnp.float32)


def spread_over(row, axis, groups=None):
    size = lax.axis_size(axis) if groups is None else len(groups[0])
    copies = jnp.broadcast_to(row[None], (size,) + row.shape)
    return lax.all_to_all(copies, axis, 0, 0, axis_index_groups=groups, tiled=True)


def local(residual, classes, class_perm, support, coarse_inverse):
    n_gx, n_gy = lax.axis_size("gx"), lax.axis_size("gy")
    near = LANES // CF
    residual, classes, support = rows_of(residual), rows_of(classes), rows_of(support)

    (message,) = call(
        coarse_kernel, [floats(n_gy, 1, LANES)], vmem(2), [residual, support], name="coarse"
    )
    payload, edge = call(
        pack_kernel,
        [floats(2 * ROWS, LANES), floats(NZ, LANES)],
        [pl.BlockSpec(memory_space=pltpu.SMEM)] + vmem(2),
        [class_perm, residual, classes],
        name="pack",
    )

    across = [[s * near + i for i in range(near)] for s in range(n_gx // near)]
    along = [[s * near + i for s in range(n_gx // near)] for i in range(near)]
    got = lax.all_to_all(message, "gy", 0, 0, tiled=True)
    row = jnp.sum(got, axis=0)
    got = spread_over(row, "gx", across).reshape(near, LANES)
    gathered = spread_over(got, "gx", along).reshape(n_gx, LANES)

    forward_y = [(i, i + 1) for i in range(n_gy - 1)]
    backward_y = [(j, i) for i, j in forward_y]
    forward_x = [(i, i + 1) for i in range(n_gx - 1)]
    backward_x = [(j, i) for i, j in forward_x]
    above = lax.ppermute(edge, "gy", backward_y)
    below = lax.ppermute(edge, "gy", forward_y)
    (own,) = call(
        merge_kernel,
        [floats(2 * ROWS + NZ, LANES)],
        vmem(3),
        [payload, above, below],
        scratch=[pltpu.SemaphoreType.DMA],
        name="merge",
    )
    low = lax.ppermute(own, "gx", forward_x)
    high = lax.ppermute(own, "gx", backward_x)
    planes = pltpu.VMEM((WIDE, TILES + 1, NZ, LANES), jnp.float32)
    (smooth,) = call(
        smooth_kernel,
        [floats(ROWS, LANES)],
        vmem(3),
        [low, own, high],
        scratch=[planes] * 7
        + [
            pltpu.VMEM((WIDE, TILES + 1, 8, LANES), jnp.float32),
            pltpu.VMEM((TILES + 1, NZ, LANES), jnp.float32),
            pltpu.VMEM((WIDE, TILES, NZ, LANES), jnp.float32),
        ],
        flops=20_000_000,
        name="smooth",
    )
    (out,) = call(
        correct_kernel,
        [floats(ROWS, LANES)],
        vmem(4),
        [gathered, coarse_inverse, support, smooth],
        name="correct",
    )
    return block_of(out)


def solution(mesh):
    return jax.shard_map(
        local,
        mesh=mesh,
        in_specs=(
            P(None, "gx", "gy"),
            P(None, "gx", "gy"),
            P(),
            P(None, "gx", "gy"),
            P(("gx", "gy"), None),
        ),
        out_specs=P(None, "gx", "gy"),
        check_vma=False,
    )
```

```python
import math

import jax
import jax.numpy as jnp
from jax import lax
from jax.experimental import pallas as pl
from jax.experimental.pallas import tpu as pltpu
from jax.sharding import PartitionSpec as P

SWEEPS = 4
LOWER, UPPER = 0.1, 2.0
CF = 16
NZ, CX, LANES = 64, 4, 128
TILES = 2
ROWS = NZ * CX * TILES
STEP = CX * TILES
GROUPS = NZ // 8
FAR_ROW = 8 * STEP
DEPTH = 4
WIDE = CX + 2 * DEPTH
STRIP = 16
OWN = 2 * ROWS + 2 * STRIP
FACE = 8
CHUNKS = 4
FAR = 10**10
NOTHING = 1e-30


def iota(shape, dim):
    return lax.broadcasted_iota(jnp.int32, shape, dim)


def inverse(value):
    return pltpu.reciprocal(value, approx=True)


def rows_of(block):
    split = block.reshape(NZ, CX, TILES, LANES)
    return split.transpose(0, 2, 1, 3).reshape(ROWS, LANES)


def block_of(rows):
    split = rows.reshape(NZ, TILES, CX, LANES)
    return split.transpose(0, 2, 1, 3).reshape(NZ, CX, TILES * LANES)


def lane_table(entry, count):
    lane = iota((8, LANES), 1)
    table = jnp.zeros((8, LANES), jnp.float32)
    for c in range(count):
        table = jnp.where(lane == c, entry(c), table)
    return table


def pick(table, index):
    return jnp.take_along_axis(table, index, axis=1, mode="promise_in_bounds")


def column_to_lanes(column, first):
    place = iota((CF, LANES), 1) == iota((CF, LANES), 0) + first
    return jnp.sum(jnp.where(place, column, 0.0), axis=0, keepdims=True)


def vector(ref, base, t, x, j):
    return ref[pl.ds(base + j * STEP + t * CX + x, 8, stride=FAR_ROW), :]


def coarse_kernel(
    perm_ref, residual_ref, support_ref, classes_ref, message_ref, own_ref,
    support_buf, classes_buf, perm_buf, sems, perm_sem, classes_sem,
):
    size = ROWS // CHUNKS
    perm_copy = pltpu.make_async_copy(perm_ref, perm_buf, perm_sem)
    classes_copy = pltpu.make_async_copy(classes_ref, classes_buf, classes_sem)

    def copies(k):
        at = pl.ds(k * size, size)
        return [
            pltpu.make_async_copy(residual_ref.at[at, :], own_ref.at[pl.ds(ROWS + k * size, size), :], sems.at[k, 0]),
            pltpu.make_async_copy(support_ref.at[at, :], support_buf.at[at, :], sems.at[k, 1]),
        ]

    perm_copy.start()
    for k in range(CHUNKS):
        for copy in copies(k):
            copy.start()
    classes_copy.start()

    def add(i, sums):
        value = own_ref[pl.ds(pl.multiple_of(ROWS + i * 8, 8), 8), :]
        which = support_buf[pl.ds(pl.multiple_of(i * 8, 8), 8), :]
        return tuple(s + jnp.where(which == c, value, 0.0) for c, s in enumerate(sums))

    sums = (jnp.zeros((8, LANES), jnp.float32),) * CF
    for k in range(CHUNKS):
        for copy in copies(k):
            copy.wait()
        sums = lax.fori_loop(k * size // 8, (k + 1) * size // 8, add, sums, unroll=4)
    rows = jnp.concatenate([jnp.sum(s, axis=0, keepdims=True) for s in sums], axis=0)
    column = jnp.sum(rows, axis=1, keepdims=True)
    row = column_to_lanes(column, lax.axis_index("gy") * CF)

    perm_copy.wait()
    table = lane_table(lambda c: 1.0 / jnp.full((8, LANES), perm_buf[c]), perm_ref.shape[0])
    classes_copy.wait()

    def look_up(i, carry):
        at = pl.ds(pl.multiple_of(i * 8, 8), 8)
        own_ref[at, :] = pick(table, classes_buf[at, :])
        return carry

    lax.fori_loop(0, ROWS // 8, look_up, 0, unroll=8)

    lane = iota((8, LANES), 1)
    for h in range(2):
        first = jnp.zeros((8, LANES), jnp.float32)
        final = jnp.zeros((8, LANES), jnp.float32)
        for g in range(GROUPS // 2):
            for item in range(2 * CX):
                low, high = (vector(own_ref, item // CX * ROWS, t, item % CX, 2 * g + h) for t in range(2))
                both = jnp.where(lane < 64, low, high)
                shift = 32 * g + 4 * item
                if shift:
                    both = pltpu.roll(both, shift, 1)
                first = jnp.where(lane // 4 == shift // 4, both, first)
                final = jnp.where((lane + 4) % LANES // 4 == shift // 4, both, final)
        me = lax.axis_index("gy")
        for k in range(message_ref.shape[0]):
            message_ref[k, FACE + 8 * h : FACE + 8 * h + 8, :] = jnp.where(me < k, final, first)
    for k in range(message_ref.shape[0]):
        message_ref[k, 0:FACE, :] = jnp.broadcast_to(row, (FACE, LANES))


def merge_kernel(got_ref, own_ref, rows_ref, out_ref):
    count = got_ref.shape[0]
    row = got_ref[0, 0:1, :]
    for k in range(1, count):
        row = row + got_ref[k, 0:1, :]
    for k in range(rows_ref.shape[0]):
        rows_ref[k] = row
    me = lax.axis_index("gy")
    strip = pl.ds(FACE, STRIP)
    above = got_ref[jnp.minimum(me + 1, count - 1), strip, :]
    below = got_ref[jnp.maximum(me - 1, 0), strip, :]
    out_ref[pl.ds(2 * ROWS, STRIP), :] = jnp.where(me < count - 1, above, 0.0)
    out_ref[pl.ds(2 * ROWS + STRIP, STRIP), :] = jnp.where(me > 0, below, 0.0)


def fan_kernel(got_ref, copies_ref):
    for k in range(copies_ref.shape[0]):
        copies_ref[k] = got_ref[...]


def smooth_kernel(low_ref, own_ref, high_ref, after_ref, out_ref, res, upd, rem, inv, tx, ty, tz, tzu, flux, total):
    middle = 0.5 * (UPPER + LOWER)
    spread = 0.5 * (UPPER - LOWER)
    sigma = middle / spread
    lane = iota((8, LANES), 1)
    low_lane = lane < 4
    halo = low_lane | (lane >= LANES - 4)
    top, bottom = iota((8, LANES), 0) == 0, iota((8, LANES), 0) == 7
    tiles = range(TILES + 1)
    groups = range(GROUPS)

    for part, ref in enumerate((low_ref, own_ref, high_ref)):
        for x in range(CX):
            i = part * CX + x
            for j in groups:
                for t in range(TILES):
                    value = vector(ref, 0, t, x, j)
                    res[i, t, j] = value if part == 1 else jnp.maximum(value, NOTHING)
                    rem[i, t, j] = 0.5 * vector(ref, ROWS, t, x, j)
                at = [pl.ds(2 * ROWS + n * STRIP + j % 2 * 8, 8) for n in range(2)]
                above, below = ref[at[0], :], ref[at[1], :]
                for a in range(2):
                    shift = 32 * (j // 2) + 4 * (CX * a + x)
                    moved = jnp.where(lane // 4 == shift // 4, above, below)
                    if shift:
                        moved = pltpu.roll(moved, LANES - shift, 1)
                    moved = jnp.where(halo, moved, 0.0)
                    if a:
                        rem[i, TILES, j] = 0.5 * moved
                    else:
                        res[i, TILES, j] = jnp.maximum(moved, NOTHING)

    def right(values):
        rolled = [pltpu.roll(v, LANES - 1, 1) for v in values]
        n = len(values)
        return [jnp.where(lane == LANES - 1, rolled[(t + 1) % n], rolled[t]) for t in range(n)]

    def left(values, count):
        rolled = [pltpu.roll(v, 1, 1) for v in values]
        return [jnp.where(lane == 0, rolled[t - 1], rolled[t]) for t in range(count)]

    def next_z(value):
        return jnp.where(bottom, 0.0, pltpu.roll(value, 7, 0))

    def last_z(value):
        return jnp.where(top, 0.0, pltpu.roll(value, 1, 0))

    for t in tiles:
        for j in groups:
            tx[0, t, j] = inverse(res[0, t, j] + res[1, t, j])

    def setup(i, carry):
        start = [res[i, t, 0] for t in tiles]
        wrap = [next_z(start[t]) for t in tiles]
        above = [inverse(start[t] + last_z(res[i, t, GROUPS - 1])) for t in tiles]
        for t in tiles:
            tzu[i, t] = above[t]
        r = start
        for j in groups:
            r_down = [res[i, t, j + 1] if j < GROUPS - 1 else wrap[t] for t in tiles]
            r_right = right(r)
            ly = [inverse(r[t] + r_right[t]) for t in tiles]
            ly_left = left(ly, TILES + 1)
            for t in tiles:
                lx = inverse(r[t] + res[i + 1, t, j])
                lz = inverse(r[t] + r_down[t])
                diagonal = ((lx + tx[i - 1, t, j]) + (ly[t] + ly_left[t])) + (lz + above[t])
                inv_diag = jnp.where(r[t] > 2 * NOTHING, inverse(diagonal), 0.0)
                tx[i, t, j], ty[i, t, j], tz[i, t, j] = lx, ly[t], lz
                inv[i, t, j] = inv_diag
                update = inv_diag * rem[i, t, j] * (1.0 / middle)
                upd[i, t, j] = update
                if t < TILES:
                    total[i, t, j] = update
                above[t] = lz
            r = r_down
        return carry

    lax.fori_loop(1, WIDE - 1, setup, 0)

    weight_old = 1.0 / sigma
    for sweep in range(1, SWEEPS):
        last = sweep == SWEEPS - 1
        begin, end = 1 + sweep, WIDE - 1 - sweep
        weight_new = 1.0 / (2.0 * sigma - weight_old)
        keep, gain = weight_new * weight_old, 2.0 * weight_new / spread
        weight_old = weight_new
        done = range(TILES) if last else tiles
        for t in done:
            for j in groups:
                flux[t, j] = tx[begin - 1, t, j] * (upd[begin - 1, t, j] - upd[begin, t, j])

        def step(i, carry):
            u = [upd[i, t, 0] for t in tiles]
            wrap = [next_z(u[t]) for t in done]
            above = [tzu[i, t] * (last_z(upd[i, t, GROUPS - 1]) - u[t]) for t in done]
            for j in groups:
                u_down = [upd[i, t, j + 1] if j < GROUPS - 1 else (wrap + u)[t] for t in tiles]
                u_right = right(u)
                fy = [ty[i, t, j] * (u[t] - u_right[t]) for t in tiles]
                fy_left = left(fy, len(done))
                for t in done:
                    fx = tx[i, t, j] * (u[t] - upd[i + 1, t, j])
                    fz = tz[i, t, j] * (u[t] - u_down[t])
                    applied = ((fx - flux[t, j]) + (fy[t] - fy_left[t])) + (fz - above[t])
                    above[t] = fz
                    flux[t, j] = fx
                    remain = rem[i, t, j] - applied
                    new = keep * u[t] + gain * inv[i, t, j] * remain
                    if last:
                        at = pl.ds(j * STEP + t * CX + i - DEPTH, 8, stride=FAR_ROW)
                        out_ref[at, :] = total[i, t, j] + new
                    else:
                        rem[i, t, j] = remain
                        upd[i, t, j] = new
                        if t < TILES:
                            total[i, t, j] = total[i, t, j] + new
                u = u_down
            return carry

        lax.fori_loop(begin, end, step, 0)


def correct_kernel(gathered_ref, inverse_ref, support_ref, smooth_ref, out_ref, buf, sems):
    zero = jnp.zeros((CF, LANES), jnp.float32)
    sums = [zero] * 4
    for q in range(gathered_ref.shape[0]):
        part = inverse_ref[:, q * LANES : (q + 1) * LANES] * gathered_ref[pl.ds(q, 1), :]
        sums[q % 4] = sums[q % 4] + part
    column = jnp.sum((sums[0] + sums[1]) + (sums[2] + sums[3]), axis=1, keepdims=True)
    table = jnp.broadcast_to(column_to_lanes(column, 0), (8, LANES))

    def step(i, carry):
        at = pl.ds(pl.multiple_of(i * 8, 8), 8)
        buf[at, :] = smooth_ref[at, :] + pick(table, support_ref[at, :])
        return carry

    size = ROWS // CHUNKS
    copies = []
    for k in range(CHUNKS):
        lax.fori_loop(k * size // 8, (k + 1) * size // 8, step, 0, unroll=8)
        at = pl.ds(k * size, size)
        copies.append(pltpu.make_async_copy(buf.at[at, :], out_ref.at[at, :], sems.at[k]))
        copies[-1].start()
    for copy in copies:
        copy.wait()


def specs(space, count=1):
    return [pl.BlockSpec(memory_space=space)] * count


def call(kernel, outs, ins, args, out_space=pltpu.VMEM, flops=0, **options):
    size = sum(a.size * 4 for a in args) + sum(math.prod(o.shape) * 4 for o in outs)
    return pl.pallas_call(
        kernel,
        out_shape=outs,
        in_specs=ins,
        out_specs=specs(out_space, len(outs)),
        compiler_params=pltpu.CompilerParams(vmem_limit_bytes=24 * 1024 * 1024),
        cost_estimate=pl.CostEstimate(flops=flops, bytes_accessed=size, transcendentals=0),
        **options,
    )(*args)


def held(*shape):
    return pltpu.VMEM(shape, jnp.float32)


def local(residual, classes, class_perm, support, coarse_inverse):
    n_gx, n_gy = lax.axis_size("gx"), lax.axis_size("gy")
    near = LANES // CF
    residual, classes, support = rows_of(residual), rows_of(classes), rows_of(support)

    message, own = call(
        coarse_kernel,
        [held(n_gy, FACE + STRIP, LANES), held(OWN, LANES)],
        specs(pltpu.HBM, 4),
        [class_perm, residual, support, classes],
        scratch_shapes=[
            pltpu.VMEM((ROWS, LANES), jnp.int32),
            pltpu.VMEM((ROWS, LANES), jnp.int32),
            pltpu.SMEM(class_perm.shape, jnp.float32),
            pltpu.SemaphoreType.DMA((CHUNKS, 2)),
            pltpu.SemaphoreType.DMA,
            pltpu.SemaphoreType.DMA,
        ],
        name="coarse",
    )
    across = [[s * near + i for i in range(near)] for s in range(n_gx // near)]
    along = [[s * near + i for s in range(n_gx // near)] for i in range(near)]
    got = lax.all_to_all(message, "gy", 0, 0, tiled=True)
    rows, own = call(
        merge_kernel,
        [held(near, 1, LANES), held(OWN, LANES)],
        specs(pltpu.VMEM, 2),
        [got, own],
        input_output_aliases={1: 1},
        name="merge",
    )
    got_x = lax.all_to_all(rows, "gx", 0, 0, axis_index_groups=across, tiled=True)
    got_x = got_x.reshape(near, LANES)
    (copies,) = call(
        fan_kernel,
        [held(n_gx // near, near, LANES)],
        specs(pltpu.VMEM),
        [got_x],
        flops=FAR,
        name="fan",
    )
    gathered = lax.all_to_all(copies, "gx", 0, 0, axis_index_groups=along, tiled=True)
    gathered = gathered.reshape(n_gx, LANES)

    forward = [(i, i + 1) for i in range(n_gx - 1)]
    backward = [(j, i) for i, j in forward]
    low = lax.ppermute(own, "gx", forward)
    high = lax.ppermute(own, "gx", backward)
    planes = pltpu.VMEM((WIDE, TILES + 1, GROUPS, 8, LANES), jnp.float32)
    (smooth,) = call(
        smooth_kernel,
        [held(ROWS, LANES)],
        specs(pltpu.VMEM, 3) + specs(pl.ANY),
        [low, own, high, got_x],
        flops=20_000_000,
        scratch_shapes=[planes] * 7
        + [
            pltpu.VMEM((WIDE, TILES + 1, 8, LANES), jnp.float32),
            pltpu.VMEM((TILES + 1, GROUPS, 8, LANES), jnp.float32),
            pltpu.VMEM((WIDE, TILES, GROUPS, 8, LANES), jnp.float32),
        ],
        name="smooth",
    )
    (out,) = call(
        correct_kernel,
        [jax.ShapeDtypeStruct((ROWS, LANES), jnp.float32)],
        specs(pltpu.VMEM, 4),
        [gathered, coarse_inverse, support, smooth],
        out_space=pltpu.HBM,
        scratch_shapes=[
            pltpu.VMEM((ROWS, LANES), jnp.float32),
            pltpu.SemaphoreType.DMA((CHUNKS,)),
        ],
        name="correct",
    )
    return block_of(out)


def solution(mesh):
    return jax.shard_map(
        local,
        mesh=mesh,
        in_specs=(
            P(None, "gx", "gy"),
            P(None, "gx", "gy"),
            P(),
            P(None, "gx", "gy"),
            P(("gx", "gy"), None),
        ),
        out_specs=P(None, "gx", "gy"),
        check_vma=False,
    )
```

```python
import math

import jax
import jax.numpy as jnp
from jax import lax
from jax.experimental import pallas as pl
from jax.experimental.pallas import tpu as pltpu
from jax.sharding import PartitionSpec as P

SWEEPS = 4
LOWER, UPPER = 0.1, 2.0
CF = 16
NZ, CX, LANES = 64, 4, 128
TILES = 2
ROWS = NZ * CX * TILES
STEP = CX * TILES
GROUPS = NZ // 8
FAR_ROW = 8 * STEP
DEPTH = 4
WIDE = CX + 2 * DEPTH
STRIP = 16
OWN = 2 * ROWS + 2 * STRIP
FACE = 8
PAD = 1
CHUNKS = 4
FAR = 10**10
NOTHING = 1e-30


def iota(shape, dim):
    return lax.broadcasted_iota(jnp.int32, shape, dim)


def inverse(value):
    return pltpu.reciprocal(value, approx=True)


def rows_of(block):
    split = block.reshape(NZ, CX, TILES, LANES)
    return split.transpose(0, 2, 1, 3).reshape(ROWS, LANES)


def block_of(rows):
    split = rows.reshape(NZ, TILES, CX, LANES)
    return split.transpose(0, 2, 1, 3).reshape(NZ, CX, TILES * LANES)


def lane_table(entry, count):
    lane = iota((8, LANES), 1)
    table = jnp.zeros((8, LANES), jnp.float32)
    for c in range(count):
        table = jnp.where(lane == c, entry(c), table)
    return table


def pick(table, index):
    return jnp.take_along_axis(table, index, axis=1, mode="promise_in_bounds")


def column_to_lanes(column, first):
    place = iota((CF, LANES), 1) == iota((CF, LANES), 0) + first
    return jnp.sum(jnp.where(place, column, 0.0), axis=0, keepdims=True)


def vector(ref, base, t, x, j):
    return ref[pl.ds(base + j * STEP + t * CX + x, 8, stride=FAR_ROW), :]


def coarse_kernel(
    perm_ref, residual_ref, support_ref, classes_ref, message_ref, own_ref,
    support_buf, classes_buf, perm_buf, sems, perm_sem, classes_sem,
):
    size = ROWS // CHUNKS
    perm_copy = pltpu.make_async_copy(perm_ref, perm_buf, perm_sem)
    classes_copy = pltpu.make_async_copy(classes_ref, classes_buf, classes_sem)

    def copies(k):
        at = pl.ds(k * size, size)
        return [
            pltpu.make_async_copy(residual_ref.at[at, :], own_ref.at[pl.ds(ROWS + k * size, size), :], sems.at[k, 0]),
            pltpu.make_async_copy(support_ref.at[at, :], support_buf.at[at, :], sems.at[k, 1]),
        ]

    perm_copy.start()
    for k in range(CHUNKS):
        for copy in copies(k):
            copy.start()
    classes_copy.start()

    def add(i, sums):
        value = own_ref[pl.ds(pl.multiple_of(ROWS + i * 8, 8), 8), :]
        which = support_buf[pl.ds(pl.multiple_of(i * 8, 8), 8), :]
        return tuple(s + jnp.where(which == c, value, 0.0) for c, s in enumerate(sums))

    sums = (jnp.zeros((8, LANES), jnp.float32),) * CF
    for k in range(CHUNKS):
        for copy in copies(k):
            copy.wait()
        sums = lax.fori_loop(k * size // 8, (k + 1) * size // 8, add, sums, unroll=4)
    rows = jnp.concatenate([jnp.sum(s, axis=0, keepdims=True) for s in sums], axis=0)
    column = jnp.sum(rows, axis=1, keepdims=True)
    row = column_to_lanes(column, lax.axis_index("gy") * CF)

    perm_copy.wait()
    table = lane_table(lambda c: 1.0 / jnp.full((8, LANES), perm_buf[c]), perm_ref.shape[0])
    classes_copy.wait()

    def look_up(i, carry):
        at = pl.ds(pl.multiple_of(i * 8, 8), 8)
        own_ref[at, :] = pick(table, classes_buf[at, :])
        return carry

    lax.fori_loop(0, ROWS // 8, look_up, 0, unroll=8)

    lane = iota((8, LANES), 1)
    for h in range(2):
        first = jnp.zeros((8, LANES), jnp.float32)
        final = jnp.zeros((8, LANES), jnp.float32)
        for g in range(GROUPS // 2):
            for item in range(2 * CX):
                low, high = (vector(own_ref, item // CX * ROWS, t, item % CX, 2 * g + h) for t in range(2))
                both = jnp.where(lane < 64, low, high)
                shift = 32 * g + 4 * item
                if shift:
                    both = pltpu.roll(both, shift, 1)
                first = jnp.where(lane // 4 == shift // 4, both, first)
                final = jnp.where((lane + 4) % LANES // 4 == shift // 4, both, final)
        me = lax.axis_index("gy")
        for k in range(message_ref.shape[0]):
            message_ref[k, FACE + 8 * h : FACE + 8 * h + 8, :] = jnp.where(me < k, final, first)
    for k in range(message_ref.shape[0]):
        message_ref[k, 0:FACE, :] = jnp.broadcast_to(row, (FACE, LANES))


def merge_kernel(got_ref, own_ref, rows_ref, out_ref):
    count = got_ref.shape[0]
    row = got_ref[0, 0:1, :]
    for k in range(1, count):
        row = row + got_ref[k, 0:1, :]
    for k in range(rows_ref.shape[0]):
        rows_ref[k] = jnp.broadcast_to(row, rows_ref.shape[1:])
    me = lax.axis_index("gy")
    strip = pl.ds(FACE, STRIP)
    above = got_ref[jnp.minimum(me + 1, count - 1), strip, :]
    below = got_ref[jnp.maximum(me - 1, 0), strip, :]
    out_ref[pl.ds(2 * ROWS, STRIP), :] = jnp.where(me < count - 1, above, 0.0)
    out_ref[pl.ds(2 * ROWS + STRIP, STRIP), :] = jnp.where(me > 0, below, 0.0)


def fan_kernel(got_ref, copies_ref):
    for k in range(copies_ref.shape[0]):
        copies_ref[k] = got_ref[:, 0, :]


def smooth_kernel(
    low_ref, own_ref, high_ref, after_ref, out_ref,
    res, upd, rem, inv, tx, ty, tyl, tz, tzu, flux, total,
):
    middle = 0.5 * (UPPER + LOWER)
    spread = 0.5 * (UPPER - LOWER)
    sigma = middle / spread
    lane = iota((8, LANES), 1)
    low_lane = lane < 4
    halo = low_lane | (lane >= LANES - 4)
    top, bottom = iota((8, LANES), 0) == 0, iota((8, LANES), 0) == 7
    tiles = range(TILES + 1)
    groups = range(GROUPS)

    for part, ref in enumerate((low_ref, own_ref, high_ref)):
        for x in range(CX):
            i = part * CX + x
            for j in groups:
                for t in range(TILES):
                    value = vector(ref, 0, t, x, j)
                    res[i, t, j] = value if part == 1 else jnp.maximum(value, NOTHING)
                    rem[i, t, j] = 0.5 * vector(ref, ROWS, t, x, j)
                above = ref[pl.ds(2 * ROWS + j % 2 * 8, 8), :]
                below = ref[pl.ds(2 * ROWS + STRIP + j % 2 * 8, 8), :]
                for a in range(2):
                    shift = 32 * (j // 2) + 4 * (CX * a + x)
                    moved = jnp.where(lane // 4 == shift // 4, above, below)
                    if shift:
                        moved = pltpu.roll(moved, LANES - shift, 1)
                    moved = jnp.where(halo, moved, 0.0)
                    if a:
                        rem[i, TILES, j] = 0.5 * moved
                    else:
                        res[i, TILES, j] = jnp.maximum(moved, NOTHING)

    def right(values):
        rolled = [pltpu.roll(v, LANES - 1, 1) for v in values]
        n = len(values)
        return [jnp.where(lane == LANES - 1, rolled[(t + 1) % n], rolled[t]) for t in range(n)]

    def left(values, count):
        rolled = [pltpu.roll(v, 1, 1) for v in values]
        return [jnp.where(lane == 0, rolled[t - 1], rolled[t]) for t in range(count)]

    def next_z(value):
        return jnp.where(bottom, 0.0, pltpu.roll(value, 7, 0))

    def last_z(value):
        return jnp.where(top, 0.0, pltpu.roll(value, 1, 0))

    for t in tiles:
        for j in groups:
            tx[0, t, j] = inverse(res[0, t, j] + res[1, t, j])

    def setup(i, carry):
        start = [res[i, t, 0] for t in tiles]
        wrap = [next_z(start[t]) for t in tiles]
        above = [inverse(start[t] + last_z(res[i, t, GROUPS - 1])) for t in tiles]
        for t in tiles:
            tzu[i, t] = above[t]
        r = start
        for j in groups:
            r_down = [res[i, t, j + 1] if j < GROUPS - 1 else wrap[t] for t in tiles]
            r_right = right(r)
            ly = [inverse(r[t] + r_right[t]) for t in tiles]
            ly_left = left(ly, TILES + 1)
            for t in tiles:
                lx = inverse(r[t] + res[i + 1, t, j])
                lz = inverse(r[t] + r_down[t])
                diagonal = ((lx + tx[i - 1, t, j]) + (ly[t] + ly_left[t])) + (lz + above[t])
                inv_diag = jnp.where(r[t] > 2 * NOTHING, inverse(diagonal), 0.0)
                tx[i, t, j], ty[i, t, j], tz[i, t, j] = lx, ly[t], lz
                tyl[i, t, j] = ly_left[t]
                inv[i, t, j] = inv_diag
                update = inv_diag * rem[i, t, j] * (1.0 / middle)
                upd[i, t, j] = update
                if t < TILES:
                    total[i, t, j] = update
                above[t] = lz
            r = r_down
        return carry

    lax.fori_loop(1, WIDE - 1, setup, 0, unroll=2)

    weight_old = 1.0 / sigma
    for sweep in range(1, SWEEPS):
        last = sweep == SWEEPS - 1
        begin, end = 1 + sweep, WIDE - 1 - sweep
        weight_new = 1.0 / (2.0 * sigma - weight_old)
        keep, gain = weight_new * weight_old, 2.0 * weight_new / spread
        weight_old = weight_new
        done = range(TILES) if last else tiles
        src, dst = (upd, res) if sweep % 2 else (res, upd)
        for t in done:
            for j in groups:
                flux[t, j] = tx[begin - 1, t, j] * (src[begin - 1, t, j] - src[begin, t, j])

        def step(i, carry):
            u = [src[i, t, 0] for t in tiles]
            wrap = [next_z(u[t]) for t in done]
            above = [tzu[i, t] * (last_z(src[i, t, GROUPS - 1]) - u[t]) for t in done]
            for j in groups:
                u_down = [src[i, t, j + 1] if j < GROUPS - 1 else (wrap + u)[t] for t in tiles]
                u_right = right(u)
                u_left = left(u, len(done))
                for t in done:
                    fx = tx[i, t, j] * (u[t] - src[i + 1, t, j])
                    fz = tz[i, t, j] * (u[t] - u_down[t])
                    applied = ((fx - flux[t, j]) + (ty[i, t, j] * (u[t] - u_right[t]) + tyl[i, t, j] * (u[t] - u_left[t]))) + (fz - above[t])
                    above[t] = fz
                    flux[t, j] = fx
                    remain = rem[i, t, j] - applied
                    new = keep * u[t] + gain * inv[i, t, j] * remain
                    if last:
                        at = pl.ds(j * STEP + t * CX + i - DEPTH, 8, stride=FAR_ROW)
                        out_ref[at, :] = total[i, t, j] + new
                    else:
                        rem[i, t, j] = remain
                        dst[i, t, j] = new
                        if t < TILES:
                            total[i, t, j] = total[i, t, j] + new
                u = u_down
            return carry

        lax.fori_loop(begin, end, step, 0, unroll=2)


def correct_kernel(gathered_ref, inverse_ref, support_ref, smooth_ref, out_ref, buf, sems):
    zero = jnp.zeros((CF, LANES), jnp.float32)
    sums = [zero] * 4
    for q in range(gathered_ref.shape[0]):
        part = inverse_ref[:, q * LANES : (q + 1) * LANES] * gathered_ref[pl.ds(q, 1), :]
        sums[q % 4] = sums[q % 4] + part
    column = jnp.sum((sums[0] + sums[1]) + (sums[2] + sums[3]), axis=1, keepdims=True)
    table = jnp.broadcast_to(column_to_lanes(column, 0), (8, LANES))

    def step(i, carry):
        at = pl.ds(pl.multiple_of(i * 8, 8), 8)
        buf[at, :] = smooth_ref[at, :] + pick(table, support_ref[at, :])
        return carry

    size = ROWS // CHUNKS
    copies = []
    for k in range(CHUNKS):
        lax.fori_loop(k * size // 8, (k + 1) * size // 8, step, 0, unroll=8)
        at = pl.ds(k * size, size)
        copies.append(pltpu.make_async_copy(buf.at[at, :], out_ref.at[at, :], sems.at[k]))
        copies[-1].start()
    for copy in copies:
        copy.wait()


def specs(space, count=1):
    return [pl.BlockSpec(memory_space=space)] * count


def call(kernel, outs, ins, args, out_space=pltpu.VMEM, flops=0, limit=24, **options):
    size = sum(a.size * 4 for a in args) + sum(math.prod(o.shape) * 4 for o in outs)
    return pl.pallas_call(
        kernel,
        out_shape=outs,
        in_specs=ins,
        out_specs=specs(out_space, len(outs)),
        compiler_params=pltpu.CompilerParams(vmem_limit_bytes=limit * 1024 * 1024),
        cost_estimate=pl.CostEstimate(flops=flops, bytes_accessed=size, transcendentals=0),
        **options,
    )(*args)


def held(*shape):
    return pltpu.VMEM(shape, jnp.float32)


def local(residual, classes, class_perm, support, coarse_inverse):
    n_gx, n_gy = lax.axis_size("gx"), lax.axis_size("gy")
    near = LANES // CF
    residual, classes, support = rows_of(residual), rows_of(classes), rows_of(support)

    message, own = call(
        coarse_kernel,
        [held(n_gy, FACE + STRIP, LANES), held(OWN, LANES)],
        specs(pltpu.HBM, 4),
        [class_perm, residual, support, classes],
        scratch_shapes=[
            pltpu.VMEM((ROWS, LANES), jnp.int32),
            pltpu.VMEM((ROWS, LANES), jnp.int32),
            pltpu.SMEM(class_perm.shape, jnp.float32),
            pltpu.SemaphoreType.DMA((CHUNKS, 2)),
            pltpu.SemaphoreType.DMA,
            pltpu.SemaphoreType.DMA,
        ],
        limit=60,
        name="coarse",
    )
    across = [[s * near + i for i in range(near)] for s in range(n_gx // near)]
    along = [[s * near + i for s in range(n_gx // near)] for i in range(near)]
    got = lax.all_to_all(message, "gy", 0, 0, tiled=True)
    rows, own = call(
        merge_kernel,
        [held(n_gx, PAD, LANES), held(OWN, LANES)],
        specs(pltpu.VMEM, 2),
        [got, own],
        input_output_aliases={1: 1},
        name="merge",
    )
    gathered = lax.all_to_all(rows, "gx", 0, 0, tiled=True).reshape(n_gx, LANES)

    forward = [(i, i + 1) for i in range(n_gx - 1)]
    backward = [(j, i) for i, j in forward]
    low = lax.ppermute(own, "gx", forward)
    high = lax.ppermute(own, "gx", backward)
    planes = pltpu.VMEM((WIDE, TILES + 1, GROUPS, 8, LANES), jnp.float32)
    (smooth,) = call(
        smooth_kernel,
        [held(ROWS, LANES)],
        specs(pltpu.VMEM, 3) + specs(pl.ANY),
        [low, own, high, rows],
        flops=20_000_000,
        scratch_shapes=[planes] * 8
        + [
            pltpu.VMEM((WIDE, TILES + 1, 8, LANES), jnp.float32),
            pltpu.VMEM((TILES + 1, GROUPS, 8, LANES), jnp.float32),
            pltpu.VMEM((WIDE, TILES, GROUPS, 8, LANES), jnp.float32),
        ],
        name="smooth",
    )
    (out,) = call(
        correct_kernel,
        [jax.ShapeDtypeStruct((ROWS, LANES), jnp.float32)],
        specs(pltpu.VMEM, 4),
        [gathered, coarse_inverse, support, smooth],
        out_space=pltpu.HBM,
        scratch_shapes=[
            pltpu.VMEM((ROWS, LANES), jnp.float32),
            pltpu.SemaphoreType.DMA((CHUNKS,)),
        ],
        name="correct",
    )
    return block_of(out)


def solution(mesh):
    return jax.shard_map(
        local,
        mesh=mesh,
        in_specs=(
            P(None, "gx", "gy"),
            P(None, "gx", "gy"),
            P(),
            P(None, "gx", "gy"),
            P(("gx", "gy"), None),
        ),
        out_specs=P(None, "gx", "gy"),
        check_vma=False,
    )
```

```python
import math

import jax
import jax.numpy as jnp
from jax import lax
from jax.experimental import pallas as pl
from jax.experimental.pallas import tpu as pltpu
from jax.sharding import PartitionSpec as P

SWEEPS = 4
LOWER, UPPER = 0.1, 2.0
CF = 16
NZ, CX, LANES = 64, 4, 128
TILES = 2
ROWS = NZ * CX * TILES
STEP = CX * TILES
GROUPS = NZ // 8
FAR_ROW = 8 * STEP
DEPTH = 4
WIDE = CX + 2 * DEPTH
STRIP = 16
SUMS = 2 * ROWS + 2 * STRIP
OWN = SUMS + 8
FACE = 8
CHUNKS = 4
NOTHING = 1e-30


def iota(shape, dim):
    return lax.broadcasted_iota(jnp.int32, shape, dim)


def inverse(value):
    return pltpu.reciprocal(value, approx=True)


def rows_of(block):
    split = block.reshape(NZ, CX, TILES, LANES)
    return split.transpose(0, 2, 1, 3).reshape(ROWS, LANES)


def block_of(rows):
    split = rows.reshape(NZ, TILES, CX, LANES)
    return split.transpose(0, 2, 1, 3).reshape(NZ, CX, TILES * LANES)


def lane_table(entry, count):
    lane = iota((8, LANES), 1)
    table = jnp.zeros((8, LANES), jnp.float32)
    for c in range(count):
        table = jnp.where(lane == c, entry(c), table)
    return table


def pick(table, index):
    return jnp.take_along_axis(table, index, axis=1, mode="promise_in_bounds")


def column_to_lanes(column, first):
    place = iota((CF, LANES), 1) == iota((CF, LANES), 0) + first
    return jnp.sum(jnp.where(place, column, 0.0), axis=0, keepdims=True)


def vector(ref, base, t, x, j):
    return ref[pl.ds(base + j * STEP + t * CX + x, 8, stride=FAR_ROW), :]


def coarse_kernel(
    perm_ref, residual_ref, support_ref, classes_ref, message_ref, own_ref,
    support_buf, classes_buf, perm_buf, sems, perm_sem, classes_sem,
):
    size = ROWS // CHUNKS
    perm_copy = pltpu.make_async_copy(perm_ref, perm_buf, perm_sem)
    classes_copy = pltpu.make_async_copy(classes_ref, classes_buf, classes_sem)

    def copies(k):
        at = pl.ds(k * size, size)
        return [
            pltpu.make_async_copy(residual_ref.at[at, :], own_ref.at[pl.ds(ROWS + k * size, size), :], sems.at[k, 0]),
            pltpu.make_async_copy(support_ref.at[at, :], support_buf.at[at, :], sems.at[k, 1]),
        ]

    perm_copy.start()
    for k in range(CHUNKS):
        for copy in copies(k):
            copy.start()
    classes_copy.start()

    def add(i, sums):
        value = own_ref[pl.ds(pl.multiple_of(ROWS + i * 8, 8), 8), :]
        which = support_buf[pl.ds(pl.multiple_of(i * 8, 8), 8), :]
        return tuple(s + jnp.where(which == c, value, 0.0) for c, s in enumerate(sums))

    sums = (jnp.zeros((8, LANES), jnp.float32),) * CF
    for k in range(CHUNKS):
        for copy in copies(k):
            copy.wait()
        sums = lax.fori_loop(k * size // 8, (k + 1) * size // 8, add, sums, unroll=4)
    rows = jnp.concatenate([jnp.sum(s, axis=0, keepdims=True) for s in sums], axis=0)
    column = jnp.sum(rows, axis=1, keepdims=True)
    row = column_to_lanes(column, lax.axis_index("gy") * CF)

    perm_copy.wait()
    table = lane_table(lambda c: 1.0 / jnp.full((8, LANES), perm_buf[c]), perm_ref.shape[0])
    classes_copy.wait()

    def look_up(i, carry):
        at = pl.ds(pl.multiple_of(i * 8, 8), 8)
        own_ref[at, :] = pick(table, classes_buf[at, :])
        return carry

    lax.fori_loop(0, ROWS // 8, look_up, 0, unroll=8)

    lane = iota((8, LANES), 1)
    for h in range(2):
        first = jnp.zeros((8, LANES), jnp.float32)
        final = jnp.zeros((8, LANES), jnp.float32)
        for g in range(GROUPS // 2):
            for item in range(2 * CX):
                low, high = (vector(own_ref, item // CX * ROWS, t, item % CX, 2 * g + h) for t in range(2))
                both = jnp.where(lane < 64, low, high)
                shift = 32 * g + 4 * item
                if shift:
                    both = pltpu.roll(both, shift, 1)
                first = jnp.where(lane // 4 == shift // 4, both, first)
                final = jnp.where((lane + 4) % LANES // 4 == shift // 4, both, final)
        me = lax.axis_index("gy")
        for k in range(message_ref.shape[0]):
            message_ref[k, FACE + 8 * h : FACE + 8 * h + 8, :] = jnp.where(me < k, final, first)
    for k in range(message_ref.shape[0]):
        message_ref[k, 0:FACE, :] = jnp.broadcast_to(row, (FACE, LANES))


def merge_kernel(got_ref, own_ref, out_ref):
    count = got_ref.shape[0]
    me = lax.axis_index("gy")
    strip = pl.ds(FACE, STRIP)
    above = got_ref[jnp.minimum(me + 1, count - 1), strip, :]
    below = got_ref[jnp.maximum(me - 1, 0), strip, :]
    out_ref[pl.ds(2 * ROWS, STRIP), :] = jnp.where(me < count - 1, above, 0.0)
    out_ref[pl.ds(2 * ROWS + STRIP, STRIP), :] = jnp.where(me > 0, below, 0.0)
    row = got_ref[0, 0:8, :]
    for k in range(1, count):
        row = row + got_ref[k, 0:8, :]
    out_ref[pl.ds(SUMS, 8), :] = row


def pair_kernel(own_ref, mate_ref, rows_ref):
    odd = lax.axis_index("gx") % 2 == 1
    own, mate = own_ref[pl.ds(SUMS, 1), :], mate_ref[pl.ds(SUMS, 1), :]
    both = jnp.concatenate([jnp.where(odd, mate, own), jnp.where(odd, own, mate)], axis=0)
    for k in range(rows_ref.shape[0]):
        rows_ref[k] = both


def smooth_kernel(
    own_ref, mate_ref, other_ref, after_ref, out_ref,
    res, upd, rem, inv, tx, ty, tyl, tz, tzu, flux, total,
):
    middle = 0.5 * (UPPER + LOWER)
    spread = 0.5 * (UPPER - LOWER)
    sigma = middle / spread
    lane = iota((8, LANES), 1)
    low_lane = lane < 4
    halo = low_lane | (lane >= LANES - 4)
    top, bottom = iota((8, LANES), 0) == 0, iota((8, LANES), 0) == 7
    tiles = range(TILES + 1)
    groups = range(GROUPS)

    odd = lax.axis_index("gx") % 2
    places = ((own_ref, DEPTH), (mate_ref, 2 * CX * (1 - odd)), (other_ref, 2 * CX * odd))
    for ref, place in places:
        for x in range(CX):
            i = place + x
            for j in groups:
                for t in range(TILES):
                    value = vector(ref, 0, t, x, j)
                    res[i, t, j] = value if ref is own_ref else jnp.maximum(value, NOTHING)
                    rem[i, t, j] = 0.5 * vector(ref, ROWS, t, x, j)
                above = ref[pl.ds(2 * ROWS + j % 2 * 8, 8), :]
                below = ref[pl.ds(2 * ROWS + STRIP + j % 2 * 8, 8), :]
                for a in range(2):
                    shift = 32 * (j // 2) + 4 * (CX * a + x)
                    moved = jnp.where(lane // 4 == shift // 4, above, below)
                    if shift:
                        moved = pltpu.roll(moved, LANES - shift, 1)
                    moved = jnp.where(halo, moved, 0.0)
                    if a:
                        rem[i, TILES, j] = 0.5 * moved
                    else:
                        res[i, TILES, j] = jnp.maximum(moved, NOTHING)

    def right(values):
        rolled = [pltpu.roll(v, LANES - 1, 1) for v in values]
        n = len(values)
        return [jnp.where(lane == LANES - 1, rolled[(t + 1) % n], rolled[t]) for t in range(n)]

    def left(values, count):
        rolled = [pltpu.roll(v, 1, 1) for v in values]
        return [jnp.where(lane == 0, rolled[t - 1], rolled[t]) for t in range(count)]

    def next_z(value):
        return jnp.where(bottom, 0.0, pltpu.roll(value, 7, 0))

    def last_z(value):
        return jnp.where(top, 0.0, pltpu.roll(value, 1, 0))

    for t in tiles:
        for j in groups:
            tx[0, t, j] = inverse(res[0, t, j] + res[1, t, j])

    def setup(i, carry):
        start = [res[i, t, 0] for t in tiles]
        wrap = [next_z(start[t]) for t in tiles]
        above = [inverse(start[t] + last_z(res[i, t, GROUPS - 1])) for t in tiles]
        for t in tiles:
            tzu[i, t] = above[t]
        r = start
        for j in groups:
            r_down = [res[i, t, j + 1] if j < GROUPS - 1 else wrap[t] for t in tiles]
            r_right = right(r)
            ly = [inverse(r[t] + r_right[t]) for t in tiles]
            ly_left = left(ly, TILES + 1)
            for t in tiles:
                lx = inverse(r[t] + res[i + 1, t, j])
                lz = inverse(r[t] + r_down[t])
                diagonal = ((lx + tx[i - 1, t, j]) + (ly[t] + ly_left[t])) + (lz + above[t])
                inv_diag = jnp.where(r[t] > 2 * NOTHING, inverse(diagonal), 0.0)
                tx[i, t, j], ty[i, t, j], tz[i, t, j] = lx, ly[t], lz
                tyl[i, t, j] = ly_left[t]
                inv[i, t, j] = inv_diag
                update = inv_diag * rem[i, t, j] * (1.0 / middle)
                upd[i, t, j] = update
                if t < TILES:
                    total[i, t, j] = update
                above[t] = lz
            r = r_down
        return carry

    lax.fori_loop(1, WIDE - 1, setup, 0, unroll=2)

    weight_old = 1.0 / sigma
    for sweep in range(1, SWEEPS):
        last = sweep == SWEEPS - 1
        begin, end = 1 + sweep, WIDE - 1 - sweep
        weight_new = 1.0 / (2.0 * sigma - weight_old)
        keep, gain = weight_new * weight_old, 2.0 * weight_new / spread
        weight_old = weight_new
        done = range(TILES) if last else tiles
        src, dst = (upd, res) if sweep % 2 else (res, upd)
        for t in done:
            for j in groups:
                flux[t, j] = tx[begin - 1, t, j] * (src[begin - 1, t, j] - src[begin, t, j])

        def step(i, carry):
            u = [src[i, t, 0] for t in tiles]
            wrap = [next_z(u[t]) for t in done]
            above = [tzu[i, t] * (last_z(src[i, t, GROUPS - 1]) - u[t]) for t in done]
            for j in groups:
                u_down = [src[i, t, j + 1] if j < GROUPS - 1 else (wrap + u)[t] for t in tiles]
                u_right = right(u)
                u_left = left(u, len(done))
                for t in done:
                    fx = tx[i, t, j] * (u[t] - src[i + 1, t, j])
                    fz = tz[i, t, j] * (u[t] - u_down[t])
                    applied = ((fx - flux[t, j]) + (ty[i, t, j] * (u[t] - u_right[t]) + tyl[i, t, j] * (u[t] - u_left[t]))) + (fz - above[t])
                    above[t] = fz
                    flux[t, j] = fx
                    remain = rem[i, t, j] - applied
                    new = keep * u[t] + gain * inv[i, t, j] * remain
                    if last:
                        at = pl.ds(j * STEP + t * CX + i - DEPTH, 8, stride=FAR_ROW)
                        out_ref[at, :] = total[i, t, j] + new
                    else:
                        rem[i, t, j] = remain
                        dst[i, t, j] = new
                        if t < TILES:
                            total[i, t, j] = total[i, t, j] + new
                u = u_down
            return carry

        lax.fori_loop(begin, end, step, 0, unroll=2)


def correct_kernel(gathered_ref, inverse_ref, support_ref, smooth_ref, out_ref, buf, sems):
    zero = jnp.zeros((CF, LANES), jnp.float32)
    sums = [zero] * 4
    for q in range(gathered_ref.shape[0]):
        part = inverse_ref[:, q * LANES : (q + 1) * LANES] * gathered_ref[pl.ds(q, 1), :]
        sums[q % 4] = sums[q % 4] + part
    column = jnp.sum((sums[0] + sums[1]) + (sums[2] + sums[3]), axis=1, keepdims=True)
    table = jnp.broadcast_to(column_to_lanes(column, 0), (8, LANES))

    def step(i, carry):
        at = pl.ds(pl.multiple_of(i * 8, 8), 8)
        buf[at, :] = smooth_ref[at, :] + pick(table, support_ref[at, :])
        return carry

    size = ROWS // CHUNKS
    copies = []
    for k in range(CHUNKS):
        lax.fori_loop(k * size // 8, (k + 1) * size // 8, step, 0, unroll=8)
        at = pl.ds(k * size, size)
        copies.append(pltpu.make_async_copy(buf.at[at, :], out_ref.at[at, :], sems.at[k]))
        copies[-1].start()
    for copy in copies:
        copy.wait()


def specs(space, count=1):
    return [pl.BlockSpec(memory_space=space)] * count


def call(kernel, outs, ins, args, out_space=pltpu.VMEM, flops=0, limit=24, **options):
    size = sum(a.size * 4 for a in args) + sum(math.prod(o.shape) * 4 for o in outs)
    return pl.pallas_call(
        kernel,
        out_shape=outs,
        in_specs=ins,
        out_specs=specs(out_space, len(outs)),
        compiler_params=pltpu.CompilerParams(vmem_limit_bytes=limit * 1024 * 1024),
        cost_estimate=pl.CostEstimate(flops=flops, bytes_accessed=size, transcendentals=0),
        **options,
    )(*args)


def held(*shape):
    return pltpu.VMEM(shape, jnp.float32)


def local(residual, classes, class_perm, support, coarse_inverse):
    n_gx, n_gy = lax.axis_size("gx"), lax.axis_size("gy")
    residual, classes, support = rows_of(residual), rows_of(classes), rows_of(support)

    message, own = call(
        coarse_kernel,
        [held(n_gy, FACE + STRIP, LANES), held(OWN, LANES)],
        specs(pltpu.HBM, 4),
        [class_perm, residual, support, classes],
        scratch_shapes=[
            pltpu.VMEM((ROWS, LANES), jnp.int32),
            pltpu.VMEM((ROWS, LANES), jnp.int32),
            pltpu.SMEM(class_perm.shape, jnp.float32),
            pltpu.SemaphoreType.DMA((CHUNKS, 2)),
            pltpu.SemaphoreType.DMA,
            pltpu.SemaphoreType.DMA,
        ],
        limit=60,
        name="coarse",
    )
    got = lax.all_to_all(message, "gy", 0, 0, tiled=True)
    (own,) = call(
        merge_kernel,
        [held(OWN, LANES)],
        specs(pltpu.VMEM, 2),
        [got, own],
        input_output_aliases={1: 0},
        name="merge",
    )
    pairs = [(i, i ^ 1) for i in range(n_gx)]
    others = [step for i in range(1, n_gx - 1, 2) for step in ((i, i + 1), (i + 1, i))]
    mate = lax.ppermute(own, "gx", pairs)
    other = lax.ppermute(own, "gx", others)
    (rows,) = call(
        pair_kernel, [held(n_gx // 2, 2, LANES)], specs(pltpu.VMEM, 2), [own, mate], name="pair"
    )
    groups = [list(range(k, n_gx, 2)) for k in range(2)]
    gathered = lax.all_to_all(rows, "gx", 0, 0, axis_index_groups=groups, tiled=True)
    gathered = gathered.reshape(n_gx, LANES)

    planes = pltpu.VMEM((WIDE, TILES + 1, GROUPS, 8, LANES), jnp.float32)
    (smooth,) = call(
        smooth_kernel,
        [held(ROWS, LANES)],
        specs(pltpu.VMEM, 3) + specs(pl.ANY),
        [own, mate, other, rows],
        flops=20_000_000,
        scratch_shapes=[planes] * 8
        + [
            pltpu.VMEM((WIDE, TILES + 1, 8, LANES), jnp.float32),
            pltpu.VMEM((TILES + 1, GROUPS, 8, LANES), jnp.float32),
            pltpu.VMEM((WIDE, TILES, GROUPS, 8, LANES), jnp.float32),
        ],
        name="smooth",
    )
    (out,) = call(
        correct_kernel,
        [jax.ShapeDtypeStruct((ROWS, LANES), jnp.float32)],
        specs(pltpu.VMEM, 4),
        [gathered, coarse_inverse, support, smooth],
        out_space=pltpu.HBM,
        scratch_shapes=[
            pltpu.VMEM((ROWS, LANES), jnp.float32),
            pltpu.SemaphoreType.DMA((CHUNKS,)),
        ],
        name="correct",
    )
    return block_of(out)


def solution(mesh):
    return jax.shard_map(
        local,
        mesh=mesh,
        in_specs=(
            P(None, "gx", "gy"),
            P(None, "gx", "gy"),
            P(),
            P(None, "gx", "gy"),
            P(("gx", "gy"), None),
        ),
        out_specs=P(None, "gx", "gy"),
        check_vma=False,
    )
```

```python
import math

import jax
import jax.numpy as jnp
from jax import lax
from jax.experimental import pallas as pl
from jax.experimental.pallas import tpu as pltpu
from jax.sharding import PartitionSpec as P

SWEEPS = 4
LOWER, UPPER = 0.1, 2.0
CF = 16
NZ, CX, LANES = 64, 4, 128
TILES = 2
ROWS = NZ * CX * TILES
STEP = CX * TILES
GROUPS = NZ // 8
FAR_ROW = 8 * STEP
DEPTH = 4
WIDE = CX + 2 * DEPTH
STRIP = 16
SUMS = 2 * ROWS + 2 * STRIP
OWN = SUMS + 8
FACE = 8
CHUNKS = 8
NOTHING = 1e-30


def iota(shape, dim):
    return lax.broadcasted_iota(jnp.int32, shape, dim)


def inverse(value):
    return pltpu.reciprocal(value, approx=True)


def rows_of(block):
    split = block.reshape(NZ, CX, TILES, LANES)
    return split.transpose(0, 2, 1, 3).reshape(ROWS, LANES)


def block_of(rows):
    split = rows.reshape(NZ, TILES, CX, LANES)
    return split.transpose(0, 2, 1, 3).reshape(NZ, CX, TILES * LANES)


def pick(entries, index):
    bit = 1
    while len(entries) > 1:
        odd = index & bit != 0
        entries = [jnp.where(odd, entries[k + 1], entries[k]) for k in range(0, len(entries), 2)]
        bit *= 2
    return entries[0]


def column_to_lanes(column, first):
    place = iota((CF, LANES), 1) == iota((CF, LANES), 0) + first
    return jnp.sum(jnp.where(place, column, 0.0), axis=0, keepdims=True)


def vector(ref, base, t, x, j):
    return ref[pl.ds(base + j * STEP + t * CX + x, 8, stride=FAR_ROW), :]


def coarse_kernel(residual_ref, support_ref, classes_ref, message_ref, own_ref, support_buf, classes_buf, sems):
    size = ROWS // CHUNKS

    def copies(k):
        at = pl.ds(k * size, size)
        return [
            pltpu.make_async_copy(residual_ref.at[at, :], own_ref.at[pl.ds(ROWS + k * size, size), :], sems.at[k, 0]),
            pltpu.make_async_copy(support_ref.at[at, :], support_buf.at[at, :], sems.at[k, 1]),
        ]

    def classes_copy(k):
        at = pl.ds(k * size, size)
        return pltpu.make_async_copy(classes_ref.at[at, :], classes_buf.at[at, :], sems.at[k, 2])

    for k in range(CHUNKS):
        for copy in copies(k):
            copy.start()
    for k in range(CHUNKS):
        classes_copy(k).start()

    def add(i, sums):
        value = own_ref[pl.ds(pl.multiple_of(ROWS + i * 8, 8), 8), :]
        which = support_buf[pl.ds(pl.multiple_of(i * 8, 8), 8), :]
        return tuple(s + jnp.where(which == c, value, 0.0) for c, s in enumerate(sums))

    sums = (jnp.zeros((8, LANES), jnp.float32),) * CF
    for k in range(CHUNKS):
        for copy in copies(k):
            copy.wait()
        sums = lax.fori_loop(k * size // 8, (k + 1) * size // 8, add, sums, unroll=8)

    def mark(i, carry):
        at = pl.ds(pl.multiple_of(i * 8, 8), 8)
        own_ref[at, :] = (classes_buf[at, :] + 1).astype(jnp.float32)
        return carry

    for k in range(CHUNKS):
        classes_copy(k).wait()
    lax.fori_loop(0, ROWS // 8, mark, 0, unroll=8)

    rows = jnp.concatenate([jnp.sum(s, axis=0, keepdims=True) for s in sums], axis=0)
    column = jnp.sum(rows, axis=1, keepdims=True)
    row = column_to_lanes(column, lax.axis_index("gy") * CF)
    for k in range(message_ref.shape[0]):
        message_ref[k, 0:FACE, :] = jnp.broadcast_to(row, (FACE, LANES))

    lane = iota((8, LANES), 1)
    me = lax.axis_index("gy")
    for h in range(2):
        first = jnp.zeros((8, LANES), jnp.float32)
        final = jnp.zeros((8, LANES), jnp.float32)
        for g in range(GROUPS // 2):
            for item in range(2 * CX):
                low, high = (vector(own_ref, item // CX * ROWS, t, item % CX, 2 * g + h) for t in range(2))
                both = jnp.where(lane < 64, low, high)
                shift = 32 * g + 4 * item
                if shift:
                    both = pltpu.roll(both, shift, 1)
                first = jnp.where(lane // 4 == shift // 4, both, first)
                final = jnp.where((lane + 4) % LANES // 4 == shift // 4, both, final)
        for k in range(message_ref.shape[0]):
            message_ref[k, FACE + 8 * h : FACE + 8 * h + 8, :] = jnp.where(me < k, final, first)


def merge_kernel(got_ref, own_ref, out_ref):
    count = got_ref.shape[0]
    me = lax.axis_index("gy")
    strip = pl.ds(FACE, STRIP)
    above = got_ref[jnp.minimum(me + 1, count - 1), strip, :]
    below = got_ref[jnp.maximum(me - 1, 0), strip, :]
    out_ref[pl.ds(2 * ROWS, STRIP), :] = jnp.where(me < count - 1, above, 0.0)
    out_ref[pl.ds(2 * ROWS + STRIP, STRIP), :] = jnp.where(me > 0, below, 0.0)
    row = got_ref[0, 0:8, :]
    for k in range(1, count):
        row = row + got_ref[k, 0:8, :]
    out_ref[pl.ds(SUMS, 8), :] = row


def pair_kernel(own_ref, mate_ref, rows_ref):
    odd = lax.axis_index("gx") % 2 == 1
    own, mate = own_ref[pl.ds(SUMS, 1), :], mate_ref[pl.ds(SUMS, 1), :]
    both = jnp.concatenate([jnp.where(odd, mate, own), jnp.where(odd, own, mate)], axis=0)
    for k in range(rows_ref.shape[0]):
        rows_ref[k] = both


def smooth_kernel(
    perm_ref, own_ref, mate_ref, other_ref, after_ref, out_ref,
    res, upd, rem, inv, tx, ty, tyl, tz, tzu, flux, total,
):
    middle = 0.5 * (UPPER + LOWER)
    spread = 0.5 * (UPPER - LOWER)
    sigma = middle / spread
    lane = iota((8, LANES), 1)
    low_lane = lane < 4
    halo = low_lane | (lane >= LANES - 4)
    top, bottom = iota((8, LANES), 0) == 0, iota((8, LANES), 0) == 7
    tiles = range(TILES + 1)
    groups = range(GROUPS)

    table = [1.0 / jnp.full((8, LANES), perm_ref[c]) for c in range(perm_ref.shape[0])]

    def resistivity(mark):
        return jnp.where(mark > 0.0, pick(table, mark.astype(jnp.int32) - 1), NOTHING)

    odd = lax.axis_index("gx") % 2
    places = ((own_ref, DEPTH), (mate_ref, 2 * CX * (1 - odd)), (other_ref, 2 * CX * odd))
    for ref, place in places:
        strips = []
        for n in range(2 * STRIP // 8):
            strip = ref[pl.ds(2 * ROWS + 8 * n, 8), :]
            marked = (lane + (4 if n >= STRIP // 8 else 0)) % 32 < 16
            mark = jnp.where(marked, strip, 0.0)
            strips.append(jnp.where(marked, resistivity(mark), 0.5 * strip))

        def unpack(x, carry):
            i = place + x
            for j in groups:
                for t in range(TILES):
                    res[i, t, j] = resistivity(vector(ref, 0, t, x, j))
                    rem[i, t, j] = 0.5 * vector(ref, ROWS, t, x, j)
                above, below = strips[j % 2], strips[2 + j % 2]
                for a, plane in enumerate((res, rem)):
                    shift = 32 * (j // 2) + 4 * (CX * a + x)
                    moved = jnp.where(lane // 4 == shift // 4, above, below)
                    moved = pltpu.roll(moved, (LANES - shift) % LANES, 1)
                    plane[i, TILES, j] = jnp.where(halo, moved, 0.0 if a else NOTHING)
            return carry

        lax.fori_loop(0, CX, unpack, 0)

    def right(values):
        rolled = [pltpu.roll(v, LANES - 1, 1) for v in values]
        n = len(values)
        return [jnp.where(lane == LANES - 1, rolled[(t + 1) % n], rolled[t]) for t in range(n)]

    def left(values, count):
        rolled = [pltpu.roll(v, 1, 1) for v in values]
        return [jnp.where(lane == 0, rolled[t - 1], rolled[t]) for t in range(count)]

    def next_z(value):
        return jnp.where(bottom, 0.0, pltpu.roll(value, 7, 0))

    def last_z(value):
        return jnp.where(top, 0.0, pltpu.roll(value, 1, 0))

    for t in tiles:
        for j in groups:
            tx[0, t, j] = inverse(res[0, t, j] + res[1, t, j])

    def setup(i, carry):
        start = [res[i, t, 0] for t in tiles]
        wrap = [next_z(start[t]) for t in tiles]
        above = [inverse(start[t] + last_z(res[i, t, GROUPS - 1])) for t in tiles]
        for t in tiles:
            tzu[i, t] = above[t]
        r = start
        for j in groups:
            r_down = [res[i, t, j + 1] if j < GROUPS - 1 else wrap[t] for t in tiles]
            r_right = right(r)
            ly = [inverse(r[t] + r_right[t]) for t in tiles]
            ly_left = left(ly, TILES + 1)
            for t in tiles:
                lx = inverse(r[t] + res[i + 1, t, j])
                lz = inverse(r[t] + r_down[t])
                diagonal = ((lx + tx[i - 1, t, j]) + (ly[t] + ly_left[t])) + (lz + above[t])
                inv_diag = jnp.where(r[t] > 2 * NOTHING, inverse(diagonal), 0.0)
                tx[i, t, j], ty[i, t, j], tz[i, t, j] = lx, ly[t], lz
                tyl[i, t, j] = ly_left[t]
                inv[i, t, j] = inv_diag
                update = inv_diag * rem[i, t, j] * (1.0 / middle)
                upd[i, t, j] = update
                if t < TILES:
                    total[i, t, j] = update
                above[t] = lz
            r = r_down
        return carry

    lax.fori_loop(1, WIDE - 1, setup, 0, unroll=2)

    weight_old = 1.0 / sigma
    for sweep in range(1, SWEEPS):
        last = sweep == SWEEPS - 1
        begin, end = 1 + sweep, WIDE - 1 - sweep
        weight_new = 1.0 / (2.0 * sigma - weight_old)
        keep, gain = weight_new * weight_old, 2.0 * weight_new / spread
        weight_old = weight_new
        done = range(TILES) if last else tiles
        src, dst = (upd, res) if sweep % 2 else (res, upd)
        for t in done:
            for j in groups:
                flux[t, j] = tx[begin - 1, t, j] * (src[begin - 1, t, j] - src[begin, t, j])

        def step(i, carry):
            u = [src[i, t, 0] for t in tiles]
            wrap = [next_z(u[t]) for t in done]
            above = [tzu[i, t] * (last_z(src[i, t, GROUPS - 1]) - u[t]) for t in done]
            for j in groups:
                u_down = [src[i, t, j + 1] if j < GROUPS - 1 else (wrap + u)[t] for t in tiles]
                u_right = right(u)
                u_left = left(u, len(done))
                for t in done:
                    fx = tx[i, t, j] * (u[t] - src[i + 1, t, j])
                    fz = tz[i, t, j] * (u[t] - u_down[t])
                    applied = ((fx - flux[t, j]) + (ty[i, t, j] * (u[t] - u_right[t]) + tyl[i, t, j] * (u[t] - u_left[t]))) + (fz - above[t])
                    above[t] = fz
                    flux[t, j] = fx
                    remain = rem[i, t, j] - applied
                    new = keep * u[t] + gain * inv[i, t, j] * remain
                    if last:
                        at = pl.ds(j * STEP + t * CX + i - DEPTH, 8, stride=FAR_ROW)
                        out_ref[at, :] = total[i, t, j] + new
                    else:
                        rem[i, t, j] = remain
                        dst[i, t, j] = new
                        if t < TILES:
                            total[i, t, j] = total[i, t, j] + new
                u = u_down
            return carry

        lax.fori_loop(begin, end, step, 0, unroll=2)


def correct_kernel(gathered_ref, inverse_ref, support_ref, smooth_ref, out_ref, buf, sems):
    zero = jnp.zeros((CF, LANES), jnp.float32)
    sums = [zero] * 4
    for q in range(gathered_ref.shape[0]):
        part = inverse_ref[:, q * LANES : (q + 1) * LANES] * gathered_ref[pl.ds(q, 1), :]
        sums[q % 4] = sums[q % 4] + part
    total = (sums[0] + sums[1]) + (sums[2] + sums[3])
    column = jnp.broadcast_to(jnp.sum(total, axis=1, keepdims=True), (CF, LANES))
    table = [jnp.broadcast_to(column[c : c + 1, :], (8, LANES)) for c in range(CF)]

    def step(i, carry):
        at = pl.ds(pl.multiple_of(i * 8, 8), 8)
        buf[at, :] = smooth_ref[at, :] + pick(table, support_ref[at, :])
        return carry

    size = ROWS // CHUNKS
    copies = []
    for k in range(CHUNKS):
        lax.fori_loop(k * size // 8, (k + 1) * size // 8, step, 0, unroll=8)
        at = pl.ds(k * size, size)
        copies.append(pltpu.make_async_copy(buf.at[at, :], out_ref.at[at, :], sems.at[k]))
        copies[-1].start()
    for copy in copies:
        copy.wait()


def specs(space, count=1):
    return [pl.BlockSpec(memory_space=space)] * count


def call(kernel, outs, ins, args, out_space=pltpu.VMEM, flops=0, limit=24, **options):
    size = sum(a.size * 4 for a in args) + sum(math.prod(o.shape) * 4 for o in outs)
    return pl.pallas_call(
        kernel,
        out_shape=outs,
        in_specs=ins,
        out_specs=specs(out_space, len(outs)),
        compiler_params=pltpu.CompilerParams(vmem_limit_bytes=limit * 1024 * 1024),
        cost_estimate=pl.CostEstimate(flops=flops, bytes_accessed=size, transcendentals=0),
        **options,
    )(*args)


def held(*shape):
    return pltpu.VMEM(shape, jnp.float32)


def local(residual, classes, class_perm, support, coarse_inverse):
    n_gx, n_gy = lax.axis_size("gx"), lax.axis_size("gy")
    residual, classes, support = rows_of(residual), rows_of(classes), rows_of(support)

    message, own = call(
        coarse_kernel,
        [held(n_gy, FACE + STRIP, LANES), held(OWN, LANES)],
        specs(pltpu.HBM, 3),
        [residual, support, classes],
        scratch_shapes=[
            pltpu.VMEM((ROWS, LANES), jnp.int32),
            pltpu.VMEM((ROWS, LANES), jnp.int32),
            pltpu.SemaphoreType.DMA((CHUNKS, 3)),
        ],
        limit=60,
        name="coarse",
    )
    got = lax.all_to_all(message, "gy", 0, 0, tiled=True)
    (own,) = call(
        merge_kernel,
        [held(OWN, LANES)],
        specs(pltpu.VMEM, 2),
        [got, own],
        input_output_aliases={1: 0},
        name="merge",
    )
    pairs = [(i, i ^ 1) for i in range(n_gx)]
    others = [step for i in range(1, n_gx - 1, 2) for step in ((i, i + 1), (i + 1, i))]
    mate = lax.ppermute(own, "gx", pairs)
    other = lax.ppermute(own, "gx", others)
    (rows,) = call(
        pair_kernel, [held(n_gx // 2, 2, LANES)], specs(pltpu.VMEM, 2), [own, mate], name="pair"
    )
    groups = [list(range(k, n_gx, 2)) for k in range(2)]
    gathered = lax.all_to_all(rows, "gx", 0, 0, axis_index_groups=groups, tiled=True)
    gathered = gathered.reshape(n_gx, LANES)

    planes = pltpu.VMEM((WIDE, TILES + 1, GROUPS, 8, LANES), jnp.float32)
    (smooth,) = call(
        smooth_kernel,
        [held(ROWS, LANES)],
        specs(pltpu.SMEM) + specs(pltpu.VMEM, 3) + specs(pl.ANY),
        [class_perm, own, mate, other, rows],
        flops=20_000_000,
        scratch_shapes=[planes] * 8
        + [
            pltpu.VMEM((WIDE, TILES + 1, 8, LANES), jnp.float32),
            pltpu.VMEM((TILES + 1, GROUPS, 8, LANES), jnp.float32),
            pltpu.VMEM((WIDE, TILES, GROUPS, 8, LANES), jnp.float32),
        ],
        name="smooth",
    )
    (out,) = call(
        correct_kernel,
        [jax.ShapeDtypeStruct((ROWS, LANES), jnp.float32)],
        specs(pltpu.VMEM, 4),
        [gathered, coarse_inverse, support, smooth],
        out_space=pltpu.HBM,
        scratch_shapes=[
            pltpu.VMEM((ROWS, LANES), jnp.float32),
            pltpu.SemaphoreType.DMA((CHUNKS,)),
        ],
        name="correct",
    )
    return block_of(out)


def solution(mesh):
    return jax.shard_map(
        local,
        mesh=mesh,
        in_specs=(
            P(None, "gx", "gy"),
            P(None, "gx", "gy"),
            P(),
            P(None, "gx", "gy"),
            P(("gx", "gy"), None),
        ),
        out_specs=P(None, "gx", "gy"),
        check_vma=False,
    )
```

```python
import math

import jax
import jax.numpy as jnp
from jax import lax
from jax.experimental import pallas as pl
from jax.experimental.pallas import tpu as pltpu
from jax.sharding import PartitionSpec as P

SWEEPS = 4
LOWER, UPPER = 0.1, 2.0
CF = 16
NZ, CX, LANES = 64, 4, 128
TILES = 2
ROWS = NZ * CX * TILES
STEP = CX * TILES
GROUPS = NZ // 8
FAR_ROW = 8 * STEP
DEPTH = 4
WIDE = CX + 2 * DEPTH
STRIP = 16
SUMS = 2 * ROWS + 2 * STRIP
OWN = SUMS + 8
FACE = 8
TURN_Y, TURN_X = 4, 32
CHUNKS = 8
NOTHING = 1e-30


def iota(shape, dim):
    return lax.broadcasted_iota(jnp.int32, shape, dim)


def inverse(value):
    return pltpu.reciprocal(value, approx=True)


def rows_of(block):
    split = block.reshape(NZ, CX, TILES, LANES)
    return split.transpose(0, 2, 1, 3).reshape(ROWS, LANES)


def block_of(rows):
    split = rows.reshape(NZ, TILES, CX, LANES)
    return split.transpose(0, 2, 1, 3).reshape(NZ, CX, TILES * LANES)


def turned(place, turn, count):
    return (place + turn + count) % count


def pick(entries, index):
    bit = 1
    while len(entries) > 1:
        odd = index & bit != 0
        entries = [jnp.where(odd, entries[k + 1], entries[k]) for k in range(0, len(entries), 2)]
        bit *= 2
    return entries[0]


def column_to_lanes(column, first):
    place = iota((CF, LANES), 1) == iota((CF, LANES), 0) + first
    return jnp.sum(jnp.where(place, column, 0.0), axis=0, keepdims=True)


def vector(ref, base, t, x, j):
    return ref[pl.ds(base + j * STEP + t * CX + x, 8, stride=FAR_ROW), :]


def coarse_kernel(residual_ref, support_ref, classes_ref, message_ref, own_ref, support_buf, classes_buf, sems):
    size = ROWS // CHUNKS

    def copies(k):
        at = pl.ds(k * size, size)
        return [
            pltpu.make_async_copy(residual_ref.at[at, :], own_ref.at[pl.ds(ROWS + k * size, size), :], sems.at[k, 0]),
            pltpu.make_async_copy(support_ref.at[at, :], support_buf.at[at, :], sems.at[k, 1]),
        ]

    def classes_copy(k):
        at = pl.ds(k * size, size)
        return pltpu.make_async_copy(classes_ref.at[at, :], classes_buf.at[at, :], sems.at[k, 2])

    for k in range(CHUNKS):
        for copy in copies(k):
            copy.start()
    for k in range(CHUNKS):
        classes_copy(k).start()

    def add(i, sums):
        value = own_ref[pl.ds(pl.multiple_of(ROWS + i * 8, 8), 8), :]
        which = support_buf[pl.ds(pl.multiple_of(i * 8, 8), 8), :]
        return tuple(s + jnp.where(which == c, value, 0.0) for c, s in enumerate(sums))

    sums = (jnp.zeros((8, LANES), jnp.float32),) * CF
    for k in range(CHUNKS):
        for copy in copies(k):
            copy.wait()
        sums = lax.fori_loop(k * size // 8, (k + 1) * size // 8, add, sums, unroll=8)

    def mark(i, carry):
        at = pl.ds(pl.multiple_of(i * 8, 8), 8)
        own_ref[at, :] = (classes_buf[at, :] + 1).astype(jnp.float32)
        return carry

    for k in range(CHUNKS):
        classes_copy(k).wait()
    lax.fori_loop(0, ROWS // 8, mark, 0, unroll=8)

    rows = jnp.concatenate([jnp.sum(s, axis=0, keepdims=True) for s in sums], axis=0)
    column = jnp.sum(rows, axis=1, keepdims=True)
    row = column_to_lanes(column, lax.axis_index("gy") * CF)
    for k in range(message_ref.shape[0]):
        message_ref[k, 0:FACE, :] = jnp.broadcast_to(row, (FACE, LANES))

    lane = iota((8, LANES), 1)
    me = lax.axis_index("gy")
    count = message_ref.shape[0]
    for h in range(2):
        first = jnp.zeros((8, LANES), jnp.float32)
        final = jnp.zeros((8, LANES), jnp.float32)
        for g in range(GROUPS // 2):
            for item in range(2 * CX):
                low, high = (vector(own_ref, item // CX * ROWS, t, item % CX, 2 * g + h) for t in range(2))
                both = jnp.where(lane < 64, low, high)
                shift = 32 * g + 4 * item
                if shift:
                    both = pltpu.roll(both, shift, 1)
                first = jnp.where(lane // 4 == shift // 4, both, first)
                final = jnp.where((lane + 4) % LANES // 4 == shift // 4, both, final)
        for k in range(message_ref.shape[0]):
            message_ref[k, FACE + 8 * h : FACE + 8 * h + 8, :] = jnp.where(me < turned(k, TURN_Y, count), final, first)


def merge_kernel(got_ref, own_ref, out_ref):
    count = got_ref.shape[0]
    me = lax.axis_index("gy")
    strip = pl.ds(FACE, STRIP)
    above = got_ref[turned(me + 1, -TURN_Y, count), strip, :]
    below = got_ref[turned(me - 1, -TURN_Y, count), strip, :]
    out_ref[pl.ds(2 * ROWS, STRIP), :] = jnp.where(me < count - 1, above, 0.0)
    out_ref[pl.ds(2 * ROWS + STRIP, STRIP), :] = jnp.where(me > 0, below, 0.0)
    row = got_ref[0, 0:8, :]
    for k in range(1, count):
        row = row + got_ref[k, 0:8, :]
    out_ref[pl.ds(SUMS, 8), :] = row


def pair_kernel(own_ref, mate_ref, rows_ref):
    odd = lax.axis_index("gx") % 2 == 1
    own, mate = own_ref[pl.ds(SUMS, 1), :], mate_ref[pl.ds(SUMS, 1), :]
    both = jnp.concatenate([jnp.where(odd, mate, own), jnp.where(odd, own, mate)], axis=0)
    for k in range(rows_ref.shape[0]):
        rows_ref[k] = both


def smooth_kernel(
    perm_ref, own_ref, mate_ref, other_ref, after_ref, out_ref,
    perm_buf, sem, res, upd, rem, inv, tx, ty, tyl, tz, tzu, flux, total,
):
    middle = 0.5 * (UPPER + LOWER)
    spread = 0.5 * (UPPER - LOWER)
    sigma = middle / spread
    lane = iota((8, LANES), 1)
    low_lane = lane < 4
    halo = low_lane | (lane >= LANES - 4)
    top, bottom = iota((8, LANES), 0) == 0, iota((8, LANES), 0) == 7
    tiles = range(TILES + 1)
    groups = range(GROUPS)

    perm_copy = pltpu.make_async_copy(perm_ref, perm_buf, sem)
    perm_copy.start()
    odd = lax.axis_index("gx") % 2
    places = ((own_ref, DEPTH), (mate_ref, 2 * CX * (1 - odd)), (other_ref, 2 * CX * odd))

    def unpack(ref, place, plane, a, change, outside):
        def one(x, carry):
            for j in groups:
                for t in range(TILES):
                    plane[place + x, t, j] = change(vector(ref, a * ROWS, t, x, j))
            return carry

        lax.fori_loop(0, CX, one, 0, unroll=2)
        strips = []
        for n in range(2 * STRIP // 8):
            strip = ref[pl.ds(2 * ROWS + 8 * n, 8), :]
            marked = (lane + (4 if n >= STRIP // 8 else 0)) % 32 < 16
            strips.append(change(jnp.where(marked, 0.0, strip) if a else jnp.where(marked, strip, 0.0)))
        for x in range(CX):
            for j in groups:
                shift = 32 * (j // 2) + 4 * (CX * a + x)
                moved = jnp.where(lane // 4 == shift // 4, strips[j % 2], strips[2 + j % 2])
                if shift:
                    moved = pltpu.roll(moved, LANES - shift, 1)
                plane[place + x, TILES, j] = jnp.where(halo, moved, outside)

    for ref, place in places:
        unpack(ref, place, rem, 1, lambda value: 0.5 * value, 0.0)
    perm_copy.wait()
    table = [1.0 / jnp.full((8, LANES), perm_buf[c]) for c in range(perm_ref.shape[0])]

    def resistivity(mark):
        return jnp.where(mark > 0.0, pick(table, mark.astype(jnp.int32) - 1), NOTHING)

    for ref, place in places:
        unpack(ref, place, res, 0, resistivity, NOTHING)

    def right(values):
        rolled = [pltpu.roll(v, LANES - 1, 1) for v in values]
        n = len(values)
        return [jnp.where(lane == LANES - 1, rolled[(t + 1) % n], rolled[t]) for t in range(n)]

    def left(values, count):
        rolled = [pltpu.roll(v, 1, 1) for v in values]
        return [jnp.where(lane == 0, rolled[t - 1], rolled[t]) for t in range(count)]

    def next_z(value):
        return jnp.where(bottom, 0.0, pltpu.roll(value, 7, 0))

    def last_z(value):
        return jnp.where(top, 0.0, pltpu.roll(value, 1, 0))

    for t in tiles:
        for j in groups:
            tx[0, t, j] = inverse(res[0, t, j] + res[1, t, j])

    def setup(i, carry):
        start = [res[i, t, 0] for t in tiles]
        wrap = [next_z(start[t]) for t in tiles]
        above = [inverse(start[t] + last_z(res[i, t, GROUPS - 1])) for t in tiles]
        for t in tiles:
            tzu[i, t] = above[t]
        r = start
        for j in groups:
            r_down = [res[i, t, j + 1] if j < GROUPS - 1 else wrap[t] for t in tiles]
            r_right = right(r)
            ly = [inverse(r[t] + r_right[t]) for t in tiles]
            ly_left = left(ly, TILES + 1)
            for t in tiles:
                lx = inverse(r[t] + res[i + 1, t, j])
                lz = inverse(r[t] + r_down[t])
                diagonal = ((lx + tx[i - 1, t, j]) + (ly[t] + ly_left[t])) + (lz + above[t])
                inv_diag = jnp.where(r[t] > 2 * NOTHING, inverse(diagonal), 0.0)
                tx[i, t, j], ty[i, t, j], tz[i, t, j] = lx, ly[t], lz
                tyl[i, t, j] = ly_left[t]
                inv[i, t, j] = inv_diag
                update = inv_diag * rem[i, t, j] * (1.0 / middle)
                upd[i, t, j] = update
                if t < TILES:
                    total[i, t, j] = update
                above[t] = lz
            r = r_down
        return carry

    lax.fori_loop(1, WIDE - 1, setup, 0, unroll=2)

    weight_old = 1.0 / sigma
    for sweep in range(1, SWEEPS):
        last = sweep == SWEEPS - 1
        begin, end = 1 + sweep, WIDE - 1 - sweep
        weight_new = 1.0 / (2.0 * sigma - weight_old)
        keep, gain = weight_new * weight_old, 2.0 * weight_new / spread
        weight_old = weight_new
        done = range(TILES) if last else tiles
        src, dst = (upd, res) if sweep % 2 else (res, upd)
        for t in done:
            for j in groups:
                flux[t, j] = tx[begin - 1, t, j] * (src[begin - 1, t, j] - src[begin, t, j])

        def step(i, carry):
            u = [src[i, t, 0] for t in tiles]
            wrap = [next_z(u[t]) for t in done]
            above = [tzu[i, t] * (last_z(src[i, t, GROUPS - 1]) - u[t]) for t in done]
            for j in groups:
                u_down = [src[i, t, j + 1] if j < GROUPS - 1 else (wrap + u)[t] for t in tiles]
                u_right = right(u)
                u_left = left(u, len(done))
                for t in done:
                    fx = tx[i, t, j] * (u[t] - src[i + 1, t, j])
                    fz = tz[i, t, j] * (u[t] - u_down[t])
                    applied = ((fx - flux[t, j]) + (ty[i, t, j] * (u[t] - u_right[t]) + tyl[i, t, j] * (u[t] - u_left[t]))) + (fz - above[t])
                    above[t] = fz
                    flux[t, j] = fx
                    remain = rem[i, t, j] - applied
                    new = keep * u[t] + gain * inv[i, t, j] * remain
                    if last:
                        at = pl.ds(j * STEP + t * CX + i - DEPTH, 8, stride=FAR_ROW)
                        out_ref[at, :] = total[i, t, j] + new
                    else:
                        rem[i, t, j] = remain
                        dst[i, t, j] = new
                        if t < TILES:
                            total[i, t, j] = total[i, t, j] + new
                u = u_down
            return carry

        lax.fori_loop(begin, end, step, 0, unroll=2)


def correct_kernel(gathered_ref, inverse_ref, support_ref, smooth_ref, out_ref, buf, sems):
    zero = jnp.zeros((CF, LANES), jnp.float32)
    sums = [zero] * 4
    count = gathered_ref.shape[0]
    for q in range(count):
        row = gathered_ref[pl.ds(turned(q, -TURN_X, count), 1), :]
        part = inverse_ref[:, q * LANES : (q + 1) * LANES] * row
        sums[q % 4] = sums[q % 4] + part
    total = (sums[0] + sums[1]) + (sums[2] + sums[3])
    column = jnp.broadcast_to(jnp.sum(total, axis=1, keepdims=True), (CF, LANES))
    table = [jnp.broadcast_to(column[c : c + 1, :], (8, LANES)) for c in range(CF)]

    def step(i, carry):
        at = pl.ds(pl.multiple_of(i * 8, 8), 8)
        buf[at, :] = smooth_ref[at, :] + pick(table, support_ref[at, :])
        return carry

    size = ROWS // CHUNKS
    copies = []
    for k in range(CHUNKS):
        lax.fori_loop(k * size // 8, (k + 1) * size // 8, step, 0, unroll=8)
        at = pl.ds(k * size, size)
        copies.append(pltpu.make_async_copy(buf.at[at, :], out_ref.at[at, :], sems.at[k]))
        copies[-1].start()
    for copy in copies:
        copy.wait()


def specs(space, count=1):
    return [pl.BlockSpec(memory_space=space)] * count


def call(kernel, outs, ins, args, out_space=pltpu.VMEM, flops=0, limit=24, **options):
    size = sum(a.size * 4 for a in args) + sum(math.prod(o.shape) * 4 for o in outs)
    return pl.pallas_call(
        kernel,
        out_shape=outs,
        in_specs=ins,
        out_specs=specs(out_space, len(outs)),
        compiler_params=pltpu.CompilerParams(vmem_limit_bytes=limit * 1024 * 1024),
        cost_estimate=pl.CostEstimate(flops=flops, bytes_accessed=size, transcendentals=0),
        **options,
    )(*args)


def held(*shape):
    return pltpu.VMEM(shape, jnp.float32)


def local(residual, classes, class_perm, support, coarse_inverse):
    n_gx, n_gy = lax.axis_size("gx"), lax.axis_size("gy")
    residual, classes, support = rows_of(residual), rows_of(classes), rows_of(support)

    message, own = call(
        coarse_kernel,
        [held(n_gy, FACE + STRIP, LANES), held(OWN, LANES)],
        specs(pltpu.HBM, 3),
        [residual, support, classes],
        scratch_shapes=[
            pltpu.VMEM((ROWS, LANES), jnp.int32),
            pltpu.VMEM((ROWS, LANES), jnp.int32),
            pltpu.SemaphoreType.DMA((CHUNKS, 3)),
        ],
        limit=60,
        name="coarse",
    )
    columns = [[turned(k, TURN_Y, n_gy) for k in range(n_gy)]]
    got = lax.all_to_all(message, "gy", 0, 0, axis_index_groups=columns, tiled=True)
    (own,) = call(
        merge_kernel,
        [held(OWN, LANES)],
        specs(pltpu.VMEM, 2),
        [got, own],
        input_output_aliases={1: 0},
        name="merge",
    )
    pairs = [(i, i ^ 1) for i in range(n_gx)]
    others = [step for i in range(1, n_gx - 1, 2) for step in ((i, i + 1), (i + 1, i))]
    mate = lax.ppermute(own, "gx", pairs)
    other = lax.ppermute(own, "gx", others)
    (rows,) = call(
        pair_kernel, [held(n_gx // 2, 2, LANES)], specs(pltpu.VMEM, 2), [own, mate], name="pair"
    )
    groups = [[turned(2 * i, TURN_X, n_gx) + k for i in range(n_gx // 2)] for k in range(2)]
    gathered = lax.all_to_all(rows, "gx", 0, 0, axis_index_groups=groups, tiled=True)
    gathered = gathered.reshape(n_gx, LANES)

    planes = pltpu.VMEM((WIDE, TILES + 1, GROUPS, 8, LANES), jnp.float32)
    (smooth,) = call(
        smooth_kernel,
        [held(ROWS, LANES)],
        specs(pltpu.HBM) + specs(pltpu.VMEM, 3) + specs(pl.ANY),
        [class_perm, own, mate, other, rows],
        flops=20_000_000,
        scratch_shapes=[pltpu.SMEM(class_perm.shape, jnp.float32), pltpu.SemaphoreType.DMA]
        + [planes] * 8
        + [
            pltpu.VMEM((WIDE, TILES + 1, 8, LANES), jnp.float32),
            pltpu.VMEM((TILES + 1, GROUPS, 8, LANES), jnp.float32),
            pltpu.VMEM((WIDE, TILES, GROUPS, 8, LANES), jnp.float32),
        ],
        name="smooth",
    )
    (out,) = call(
        correct_kernel,
        [jax.ShapeDtypeStruct((ROWS, LANES), jnp.float32)],
        specs(pltpu.VMEM, 4),
        [gathered, coarse_inverse, support, smooth],
        out_space=pltpu.HBM,
        scratch_shapes=[
            pltpu.VMEM((ROWS, LANES), jnp.float32),
            pltpu.SemaphoreType.DMA((CHUNKS,)),
        ],
        name="correct",
    )
    return block_of(out)


def solution(mesh):
    return jax.shard_map(
        local,
        mesh=mesh,
        in_specs=(
            P(None, "gx", "gy"),
            P(None, "gx", "gy"),
            P(),
            P(None, "gx", "gy"),
            P(("gx", "gy"), None),
        ),
        out_specs=P(None, "gx", "gy"),
        check_vma=False,
    )
```

```python
import math

import jax
import jax.numpy as jnp
from jax import lax
from jax.experimental import pallas as pl
from jax.experimental.pallas import tpu as pltpu
from jax.sharding import PartitionSpec as P

SWEEPS = 4
LOWER, UPPER = 0.1, 2.0
CF = 16
NZ, CX, LANES = 64, 4, 128
TILES = 2
ROWS = NZ * CX * TILES
STEP = CX * TILES
GROUPS = NZ // 8
FAR_ROW = 8 * STEP
DEPTH = 4
WIDE = CX + 2 * DEPTH
STRIP = 16
SUMS = 2 * ROWS + 2 * STRIP
OWN = SUMS + 8
SPARE = 96
TURN_Y, TURN_X = 4, 32
CHUNKS = 8
NOTHING = 1e-30


def iota(shape, dim):
    return lax.broadcasted_iota(jnp.int32, shape, dim)


def inverse(value):
    return pltpu.reciprocal(value, approx=True)


def rows_of(block):
    split = block.reshape(NZ, CX, TILES, LANES)
    return split.transpose(0, 2, 1, 3).reshape(ROWS, LANES)


def block_of(rows):
    split = rows.reshape(NZ, TILES, CX, LANES)
    return split.transpose(0, 2, 1, 3).reshape(NZ, CX, TILES * LANES)


def within(lane, first, count):
    return (lane >= first) & (lane < first + count)


def turned(place, turn, count):
    return (place + turn + count) % count


def pick(entries, index):
    bit = 1
    while len(entries) > 1:
        odd = index & bit != 0
        entries = [jnp.where(odd, entries[k + 1], entries[k]) for k in range(0, len(entries), 2)]
        bit *= 2
    return entries[0]


def column_to_lanes(column, first):
    place = iota((CF, LANES), 1) == iota((CF, LANES), 0) + first
    return jnp.sum(jnp.where(place, column, 0.0), axis=0, keepdims=True)


def vector(ref, base, t, x, j):
    return ref[pl.ds(base + j * STEP + t * CX + x, 8, stride=FAR_ROW), :]


def coarse_kernel(
    perm_ref, residual_ref, support_ref, classes_ref, message_ref, own_ref,
    perm_buf, support_buf, classes_buf, perm_sem, sems,
):
    size = ROWS // CHUNKS

    def copies(k):
        at = pl.ds(k * size, size)
        return [
            pltpu.make_async_copy(residual_ref.at[at, :], own_ref.at[pl.ds(ROWS + k * size, size), :], sems.at[k, 0]),
            pltpu.make_async_copy(support_ref.at[at, :], support_buf.at[at, :], sems.at[k, 1]),
        ]

    def classes_copy(k):
        at = pl.ds(k * size, size)
        return pltpu.make_async_copy(classes_ref.at[at, :], classes_buf.at[at, :], sems.at[k, 2])

    perm_copy = pltpu.make_async_copy(perm_ref, perm_buf, perm_sem)
    perm_copy.start()
    for k in range(CHUNKS):
        for copy in copies(k):
            copy.start()
    for k in range(CHUNKS):
        classes_copy(k).start()

    def add(i, sums):
        value = own_ref[pl.ds(pl.multiple_of(ROWS + i * 8, 8), 8), :]
        which = support_buf[pl.ds(pl.multiple_of(i * 8, 8), 8), :]
        return tuple(s + jnp.where(which == c, value, 0.0) for c, s in enumerate(sums))

    sums = (jnp.zeros((8, LANES), jnp.float32),) * CF
    for k in range(CHUNKS):
        for copy in copies(k):
            copy.wait()
        sums = lax.fori_loop(k * size // 8, (k + 1) * size // 8, add, sums, unroll=8)

    perm_copy.wait()
    table = [1.0 / jnp.full((8, LANES), perm_buf[c]) for c in range(perm_ref.shape[0])]

    def look_up(i, carry):
        at = pl.ds(pl.multiple_of(i * 8, 8), 8)
        own_ref[at, :] = pick(table, classes_buf[at, :])
        return carry

    for k in range(CHUNKS):
        classes_copy(k).wait()
    lax.fori_loop(0, ROWS // 8, look_up, 0, unroll=4)

    rows = jnp.concatenate([jnp.sum(s, axis=0, keepdims=True) for s in sums], axis=0)
    column = jnp.sum(rows, axis=1, keepdims=True)
    row = column_to_lanes(column, SPARE)

    lane = iota((8, LANES), 1)
    me = lax.axis_index("gy")
    count = message_ref.shape[0]
    for a in range(2):
        width = DEPTH - a
        first = final = jnp.zeros((8, LANES), jnp.float32)
        for j in range(GROUPS):
            for x in range(CX):
                both = jnp.where(lane < 64, vector(own_ref, a * ROWS, 0, x, j), vector(own_ref, a * ROWS, 1, x, j))
                shift = width * (CX * j + x)
                if shift:
                    both = pltpu.roll(both, shift, 1)
                first = jnp.where(within(lane, shift, width), both, first)
                final = jnp.where(within(lane, (shift - width) % LANES, width), both, final)
        for k in range(count):
            strip = jnp.where(me < turned(k, TURN_Y, count), final, first)
            if a:
                strip = jnp.where(within(lane, SPARE, CF), row, strip)
            message_ref[k, 8 * a : 8 * a + 8, :] = strip


def merge_kernel(got_ref, own_ref, out_ref):
    count = got_ref.shape[0]
    me = lax.axis_index("gy")
    above = got_ref[turned(me + 1, -TURN_Y, count)]
    below = got_ref[turned(me - 1, -TURN_Y, count)]
    out_ref[pl.ds(2 * ROWS, STRIP), :] = jnp.where(me < count - 1, above, 0.0)
    out_ref[pl.ds(2 * ROWS + STRIP, STRIP), :] = jnp.where(me > 0, below, 0.0)
    lane = iota((8, LANES), 1)
    row = jnp.zeros((8, LANES), jnp.float32)
    for k in range(count):
        first = CF * turned(k, TURN_Y, count)
        moved = pltpu.roll(got_ref[k, 8:16, :], (first - SPARE) % LANES, 1) if first != SPARE else got_ref[k, 8:16, :]
        row = jnp.where(within(lane, first, CF), moved, row)
    out_ref[pl.ds(SUMS, 8), :] = row


def pair_kernel(own_ref, mate_ref, rows_ref):
    odd = lax.axis_index("gx") % 2 == 1
    own, mate = own_ref[pl.ds(SUMS, 1), :], mate_ref[pl.ds(SUMS, 1), :]
    both = jnp.concatenate([jnp.where(odd, mate, own), jnp.where(odd, own, mate)], axis=0)
    for k in range(rows_ref.shape[0]):
        rows_ref[k] = both


def smooth_kernel(
    own_ref, mate_ref, other_ref, after_ref, out_ref,
    res, upd, rem, inv, tx, ty, tyl, tz, tzu, flux, total,
):
    middle = 0.5 * (UPPER + LOWER)
    spread = 0.5 * (UPPER - LOWER)
    sigma = middle / spread
    lane = iota((8, LANES), 1)
    top, bottom = iota((8, LANES), 0) == 0, iota((8, LANES), 0) == 7
    tiles = range(TILES + 1)
    groups = range(GROUPS)

    odd = lax.axis_index("gx") % 2
    places = ((own_ref, DEPTH), (mate_ref, 2 * CX * (1 - odd)), (other_ref, 2 * CX * odd))

    for ref, place in places:
        faces = [[ref[pl.ds(2 * ROWS + 8 * n, 8), :] for n in (a, a + 2)] for a in range(2)]
        for x in range(CX):
            i = place + x
            for j in groups:
                for t in range(TILES):
                    value = vector(ref, 0, t, x, j)
                    res[i, t, j] = value if ref is own_ref else jnp.maximum(value, NOTHING)
                    rem[i, t, j] = 0.5 * vector(ref, ROWS, t, x, j)
                beyond = []
                for a, (above, below) in enumerate(faces):
                    width = DEPTH - a
                    shift = width * (CX * j + x)
                    moved = jnp.where(within(lane, shift, width), above, below)
                    if shift:
                        moved = pltpu.roll(moved, LANES - shift, 1)
                    halo = within(lane, 0, width) | within(lane, LANES - width, width)
                    beyond.append(jnp.where(halo, moved, 0.0))
                res[i, TILES, j] = jnp.maximum(beyond[0], NOTHING)
                rem[i, TILES, j] = 0.5 * beyond[1]

    def right(values):
        rolled = [pltpu.roll(v, LANES - 1, 1) for v in values]
        n = len(values)
        return [jnp.where(lane == LANES - 1, rolled[(t + 1) % n], rolled[t]) for t in range(n)]

    def left(values, count):
        rolled = [pltpu.roll(v, 1, 1) for v in values]
        return [jnp.where(lane == 0, rolled[t - 1], rolled[t]) for t in range(count)]

    def next_z(value):
        return jnp.where(bottom, 0.0, pltpu.roll(value, 7, 0))

    def last_z(value):
        return jnp.where(top, 0.0, pltpu.roll(value, 1, 0))

    for t in tiles:
        for j in groups:
            tx[0, t, j] = inverse(res[0, t, j] + res[1, t, j])

    def setup(i, carry):
        start = [res[i, t, 0] for t in tiles]
        wrap = [next_z(start[t]) for t in tiles]
        above = [inverse(start[t] + last_z(res[i, t, GROUPS - 1])) for t in tiles]
        for t in tiles:
            tzu[i, t] = above[t]
        r = start
        for j in groups:
            r_down = [res[i, t, j + 1] if j < GROUPS - 1 else wrap[t] for t in tiles]
            r_right = right(r)
            ly = [inverse(r[t] + r_right[t]) for t in tiles]
            ly_left = left(ly, TILES + 1)
            for t in tiles:
                lx = inverse(r[t] + res[i + 1, t, j])
                lz = inverse(r[t] + r_down[t])
                diagonal = ((lx + tx[i - 1, t, j]) + (ly[t] + ly_left[t])) + (lz + above[t])
                inv_diag = jnp.where(r[t] > 2 * NOTHING, inverse(diagonal), 0.0)
                tx[i, t, j], ty[i, t, j], tz[i, t, j] = lx, ly[t], lz
                tyl[i, t, j] = ly_left[t]
                inv[i, t, j] = inv_diag
                update = inv_diag * rem[i, t, j] * (1.0 / middle)
                upd[i, t, j] = update
                if t < TILES:
                    total[i, t, j] = update
                above[t] = lz
            r = r_down
        return carry

    lax.fori_loop(1, WIDE - 1, setup, 0, unroll=2)

    weight_old = 1.0 / sigma
    for sweep in range(1, SWEEPS):
        last = sweep == SWEEPS - 1
        begin, end = 1 + sweep, WIDE - 1 - sweep
        weight_new = 1.0 / (2.0 * sigma - weight_old)
        keep, gain = weight_new * weight_old, 2.0 * weight_new / spread
        weight_old = weight_new
        done = range(TILES) if last else tiles
        src, dst = (upd, res) if sweep % 2 else (res, upd)
        for t in done:
            for j in groups:
                flux[t, j] = tx[begin - 1, t, j] * (src[begin - 1, t, j] - src[begin, t, j])

        def step(i, carry):
            u = [src[i, t, 0] for t in tiles]
            wrap = [next_z(u[t]) for t in done]
            above = [tzu[i, t] * (last_z(src[i, t, GROUPS - 1]) - u[t]) for t in done]
            for j in groups:
                u_down = [src[i, t, j + 1] if j < GROUPS - 1 else (wrap + u)[t] for t in tiles]
                u_right = right(u)
                u_left = left(u, len(done))
                for t in done:
                    fx = tx[i, t, j] * (u[t] - src[i + 1, t, j])
                    fz = tz[i, t, j] * (u[t] - u_down[t])
                    applied = ((fx - flux[t, j]) + (ty[i, t, j] * (u[t] - u_right[t]) + tyl[i, t, j] * (u[t] - u_left[t]))) + (fz - above[t])
                    above[t] = fz
                    flux[t, j] = fx
                    remain = rem[i, t, j] - applied
                    new = keep * u[t] + gain * inv[i, t, j] * remain
                    if last:
                        at = pl.ds(j * STEP + t * CX + i - DEPTH, 8, stride=FAR_ROW)
                        out_ref[at, :] = total[i, t, j] + new
                    else:
                        rem[i, t, j] = remain
                        dst[i, t, j] = new
                        if t < TILES:
                            total[i, t, j] = total[i, t, j] + new
                u = u_down
            return carry

        lax.fori_loop(begin, end, step, 0, unroll=2)


def correct_kernel(gathered_ref, inverse_ref, support_ref, smooth_ref, out_ref, buf, sems):
    zero = jnp.zeros((CF, LANES), jnp.float32)
    sums = [zero] * 4
    count = gathered_ref.shape[0]
    for q in range(count):
        row = gathered_ref[pl.ds(turned(q, -TURN_X, count), 1), :]
        part = inverse_ref[:, q * LANES : (q + 1) * LANES] * row
        sums[q % 4] = sums[q % 4] + part
    total = (sums[0] + sums[1]) + (sums[2] + sums[3])
    column = jnp.broadcast_to(jnp.sum(total, axis=1, keepdims=True), (CF, LANES))
    table = [jnp.broadcast_to(column[c : c + 1, :], (8, LANES)) for c in range(CF)]

    def step(i, carry):
        at = pl.ds(pl.multiple_of(i * 8, 8), 8)
        buf[at, :] = smooth_ref[at, :] + pick(table, support_ref[at, :])
        return carry

    size = ROWS // CHUNKS
    copies = []
    for k in range(CHUNKS):
        lax.fori_loop(k * size // 8, (k + 1) * size // 8, step, 0, unroll=8)
        at = pl.ds(k * size, size)
        copies.append(pltpu.make_async_copy(buf.at[at, :], out_ref.at[at, :], sems.at[k]))
        copies[-1].start()
    for copy in copies:
        copy.wait()


def specs(space, count=1):
    return [pl.BlockSpec(memory_space=space)] * count


def call(kernel, outs, ins, args, out_space=pltpu.VMEM, flops=0, limit=24, **options):
    size = sum(a.size * 4 for a in args) + sum(math.prod(o.shape) * 4 for o in outs)
    return pl.pallas_call(
        kernel,
        out_shape=outs,
        in_specs=ins,
        out_specs=specs(out_space, len(outs)),
        compiler_params=pltpu.CompilerParams(vmem_limit_bytes=limit * 1024 * 1024),
        cost_estimate=pl.CostEstimate(flops=flops, bytes_accessed=size, transcendentals=0),
        **options,
    )(*args)


def held(*shape):
    return pltpu.VMEM(shape, jnp.float32)


def local(residual, classes, class_perm, support, coarse_inverse):
    n_gx, n_gy = lax.axis_size("gx"), lax.axis_size("gy")
    residual, classes, support = rows_of(residual), rows_of(classes), rows_of(support)

    message, own = call(
        coarse_kernel,
        [held(n_gy, STRIP, LANES), held(OWN, LANES)],
        specs(pltpu.HBM, 4),
        [class_perm, residual, support, classes],
        scratch_shapes=[
            pltpu.SMEM(class_perm.shape, jnp.float32),
            pltpu.VMEM((ROWS, LANES), jnp.int32),
            pltpu.VMEM((ROWS, LANES), jnp.int32),
            pltpu.SemaphoreType.DMA,
            pltpu.SemaphoreType.DMA((CHUNKS, 3)),
        ],
        limit=60,
        name="coarse",
    )
    columns = [[turned(k, TURN_Y, n_gy) for k in range(n_gy)]]
    got = lax.all_to_all(message, "gy", 0, 0, axis_index_groups=columns, tiled=True)
    (own,) = call(
        merge_kernel,
        [held(OWN, LANES)],
        specs(pltpu.VMEM, 2),
        [got, own],
        input_output_aliases={1: 0},
        name="merge",
    )
    pairs = [(i, i ^ 1) for i in range(n_gx)]
    others = [step for i in range(1, n_gx - 1, 2) for step in ((i, i + 1), (i + 1, i))]
    mate = lax.ppermute(own, "gx", pairs)
    other = lax.ppermute(own, "gx", others)
    (rows,) = call(
        pair_kernel, [held(n_gx // 2, 2, LANES)], specs(pltpu.VMEM, 2), [own, mate], name="pair"
    )
    groups = [[turned(2 * i, TURN_X, n_gx) + k for i in range(n_gx // 2)] for k in range(2)]
    gathered = lax.all_to_all(rows, "gx", 0, 0, axis_index_groups=groups, tiled=True)
    gathered = gathered.reshape(n_gx, LANES)

    planes = pltpu.VMEM((WIDE, TILES + 1, GROUPS, 8, LANES), jnp.float32)
    (smooth,) = call(
        smooth_kernel,
        [held(ROWS, LANES)],
        specs(pltpu.VMEM, 3) + specs(pl.ANY),
        [own, mate, other, rows],
        flops=20_000_000,
        scratch_shapes=[planes] * 8
        + [
            pltpu.VMEM((WIDE, TILES + 1, 8, LANES), jnp.float32),
            pltpu.VMEM((TILES + 1, GROUPS, 8, LANES), jnp.float32),
            pltpu.VMEM((WIDE, TILES, GROUPS, 8, LANES), jnp.float32),
        ],
        name="smooth",
    )
    (out,) = call(
        correct_kernel,
        [jax.ShapeDtypeStruct((ROWS, LANES), jnp.float32)],
        specs(pltpu.VMEM, 4),
        [gathered, coarse_inverse, support, smooth],
        out_space=pltpu.HBM,
        scratch_shapes=[
            pltpu.VMEM((ROWS, LANES), jnp.float32),
            pltpu.SemaphoreType.DMA((CHUNKS,)),
        ],
        name="correct",
    )
    return block_of(out)


def solution(mesh):
    return jax.shard_map(
        local,
        mesh=mesh,
        in_specs=(
            P(None, "gx", "gy"),
            P(None, "gx", "gy"),
            P(),
            P(None, "gx", "gy"),
            P(("gx", "gy"), None),
        ),
        out_specs=P(None, "gx", "gy"),
        check_vma=False,
    )
```

```python
import math

import jax
import jax.numpy as jnp
from jax import lax
from jax.experimental import pallas as pl
from jax.experimental.pallas import tpu as pltpu
from jax.sharding import PartitionSpec as P

SWEEPS = 4
LOWER, UPPER = 0.1, 2.0
CF = 16
NZ, CX, LANES = 64, 4, 128
TILES = 2
ROWS = NZ * CX * TILES
STEP = CX * TILES
GROUPS = NZ // 8
FAR_ROW = 8 * STEP
DEPTH = 4
WIDE = CX + 2 * DEPTH
STRIP = 16
SUMS = 2 * ROWS + 2 * STRIP
OWN = SUMS + 8
SPARE = 96
TURN_Y = 4
CHUNKS = 8
NOTHING = 1e-30


def iota(shape, dim):
    return lax.broadcasted_iota(jnp.int32, shape, dim)


def inverse(value):
    return pltpu.reciprocal(value, approx=True)


def rows_of(block):
    split = block.reshape(NZ, CX, TILES, LANES)
    return split.transpose(0, 2, 1, 3).reshape(ROWS, LANES)


def block_of(rows):
    split = rows.reshape(NZ, TILES, CX, LANES)
    return split.transpose(0, 2, 1, 3).reshape(NZ, CX, TILES * LANES)


def within(lane, first, count):
    return (lane >= first) & (lane < first + count)


def turned(place, turn, count):
    return (place + turn + count) % count


def pair_order(count):
    return [4 * ((y + 4) % 8) + 3 - x for y in range(8) for x in range(4)]


def pick(entries, index):
    bit = 1
    while len(entries) > 1:
        odd = index & bit != 0
        entries = [jnp.where(odd, entries[k + 1], entries[k]) for k in range(0, len(entries), 2)]
        bit *= 2
    return entries[0]


def column_to_lanes(column, first):
    place = iota((CF, LANES), 1) == iota((CF, LANES), 0) + first
    return jnp.sum(jnp.where(place, column, 0.0), axis=0, keepdims=True)


def vector(ref, base, t, x, j):
    return ref[pl.ds(base + j * STEP + t * CX + x, 8, stride=FAR_ROW), :]


def coarse_kernel(
    perm_ref, residual_ref, support_ref, classes_ref, message_ref, own_ref,
    perm_buf, support_buf, classes_buf, perm_sem, sems,
):
    size = ROWS // CHUNKS

    def copies(k):
        at = pl.ds(k * size, size)
        return [
            pltpu.make_async_copy(residual_ref.at[at, :], own_ref.at[pl.ds(ROWS + k * size, size), :], sems.at[k, 0]),
            pltpu.make_async_copy(support_ref.at[at, :], support_buf.at[at, :], sems.at[k, 1]),
        ]

    def classes_copy(k):
        at = pl.ds(k * size, size)
        return pltpu.make_async_copy(classes_ref.at[at, :], classes_buf.at[at, :], sems.at[k, 2])

    perm_copy = pltpu.make_async_copy(perm_ref, perm_buf, perm_sem)
    perm_copy.start()
    for k in range(CHUNKS):
        for copy in copies(k):
            copy.start()
    for k in range(CHUNKS):
        classes_copy(k).start()

    def add(i, sums):
        value = own_ref[pl.ds(pl.multiple_of(ROWS + i * 8, 8), 8), :]
        which = support_buf[pl.ds(pl.multiple_of(i * 8, 8), 8), :]
        return tuple(s + jnp.where(which == c, value, 0.0) for c, s in enumerate(sums))

    sums = (jnp.zeros((8, LANES), jnp.float32),) * CF
    for k in range(CHUNKS):
        for copy in copies(k):
            copy.wait()
        sums = lax.fori_loop(k * size // 8, (k + 1) * size // 8, add, sums, unroll=8)

    perm_copy.wait()
    table = [1.0 / jnp.full((8, LANES), perm_buf[c]) for c in range(perm_ref.shape[0])]

    def look_up(i, carry):
        at = pl.ds(pl.multiple_of(i * 8, 8), 8)
        own_ref[at, :] = pick(table, classes_buf[at, :])
        return carry

    for k in range(CHUNKS):
        classes_copy(k).wait()
    lax.fori_loop(0, ROWS // 8, look_up, 0, unroll=4)

    rows = jnp.concatenate([jnp.sum(s, axis=0, keepdims=True) for s in sums], axis=0)
    column = jnp.sum(rows, axis=1, keepdims=True)
    row = column_to_lanes(column, SPARE)

    lane = iota((8, LANES), 1)
    me = lax.axis_index("gy")
    count = message_ref.shape[0]
    for a in range(2):
        width = DEPTH - a
        first = final = jnp.zeros((8, LANES), jnp.float32)
        for j in range(GROUPS):
            for x in range(CX):
                both = jnp.where(lane < 64, vector(own_ref, a * ROWS, 0, x, j), vector(own_ref, a * ROWS, 1, x, j))
                shift = width * (CX * j + x)
                if shift:
                    both = pltpu.roll(both, shift, 1)
                first = jnp.where(within(lane, shift, width), both, first)
                final = jnp.where(within(lane, (shift - width) % LANES, width), both, final)
        for k in range(count):
            strip = jnp.where(me < turned(k, TURN_Y, count), final, first)
            if a:
                strip = jnp.where(within(lane, SPARE, CF), row, strip)
            message_ref[k, 8 * a : 8 * a + 8, :] = strip


def merge_kernel(got_ref, own_ref, out_ref):
    count = got_ref.shape[0]
    me = lax.axis_index("gy")
    above = got_ref[turned(me + 1, -TURN_Y, count)]
    below = got_ref[turned(me - 1, -TURN_Y, count)]
    out_ref[pl.ds(2 * ROWS, STRIP), :] = jnp.where(me < count - 1, above, 0.0)
    out_ref[pl.ds(2 * ROWS + STRIP, STRIP), :] = jnp.where(me > 0, below, 0.0)
    lane = iota((8, LANES), 1)
    row = jnp.zeros((8, LANES), jnp.float32)
    for k in range(count):
        first = CF * turned(k, TURN_Y, count)
        moved = pltpu.roll(got_ref[k, 8:16, :], (first - SPARE) % LANES, 1) if first != SPARE else got_ref[k, 8:16, :]
        row = jnp.where(within(lane, first, CF), moved, row)
    out_ref[pl.ds(SUMS, 8), :] = row


def pair_kernel(own_ref, mate_ref, rows_ref):
    odd = lax.axis_index("gx") % 2 == 1
    own, mate = own_ref[pl.ds(SUMS, 1), :], mate_ref[pl.ds(SUMS, 1), :]
    both = jnp.concatenate([jnp.where(odd, mate, own), jnp.where(odd, own, mate)], axis=0)
    for k in range(rows_ref.shape[0]):
        rows_ref[k] = both


def smooth_kernel(
    own_ref, mate_ref, other_ref, after_ref, out_ref,
    res, upd, rem, inv, tx, ty, tyl, tz, tzu, flux, total,
):
    middle = 0.5 * (UPPER + LOWER)
    spread = 0.5 * (UPPER - LOWER)
    sigma = middle / spread
    lane = iota((8, LANES), 1)
    top, bottom = iota((8, LANES), 0) == 0, iota((8, LANES), 0) == 7
    tiles = range(TILES + 1)
    groups = range(GROUPS)

    odd = lax.axis_index("gx") % 2
    places = ((own_ref, DEPTH), (mate_ref, 2 * CX * (1 - odd)), (other_ref, 2 * CX * odd))

    for ref, place in places:
        faces = [[ref[pl.ds(2 * ROWS + 8 * n, 8), :] for n in (a, a + 2)] for a in range(2)]
        for x in range(CX):
            i = place + x
            for j in groups:
                for t in range(TILES):
                    value = vector(ref, 0, t, x, j)
                    res[i, t, j] = value if ref is own_ref else jnp.maximum(value, NOTHING)
                    rem[i, t, j] = 0.5 * vector(ref, ROWS, t, x, j)
                beyond = []
                for a, (above, below) in enumerate(faces):
                    width = DEPTH - a
                    shift = width * (CX * j + x)
                    moved = jnp.where(within(lane, shift, width), above, below)
                    if shift:
                        moved = pltpu.roll(moved, LANES - shift, 1)
                    halo = within(lane, 0, width) | within(lane, LANES - width, width)
                    beyond.append(jnp.where(halo, moved, 0.0))
                res[i, TILES, j] = jnp.maximum(beyond[0], NOTHING)
                rem[i, TILES, j] = 0.5 * beyond[1]

    def right(values):
        rolled = [pltpu.roll(v, LANES - 1, 1) for v in values]
        n = len(values)
        return [jnp.where(lane == LANES - 1, rolled[(t + 1) % n], rolled[t]) for t in range(n)]

    def left(values, count):
        rolled = [pltpu.roll(v, 1, 1) for v in values]
        return [jnp.where(lane == 0, rolled[t - 1], rolled[t]) for t in range(count)]

    def next_z(value):
        return jnp.where(bottom, 0.0, pltpu.roll(value, 7, 0))

    def last_z(value):
        return jnp.where(top, 0.0, pltpu.roll(value, 1, 0))

    for t in tiles:
        for j in groups:
            tx[0, t, j] = inverse(res[0, t, j] + res[1, t, j])

    def setup(i, carry):
        start = [res[i, t, 0] for t in tiles]
        wrap = [next_z(start[t]) for t in tiles]
        above = [inverse(start[t] + last_z(res[i, t, GROUPS - 1])) for t in tiles]
        for t in tiles:
            tzu[i, t] = above[t]
        r = start
        for j in groups:
            r_down = [res[i, t, j + 1] if j < GROUPS - 1 else wrap[t] for t in tiles]
            r_right = right(r)
            ly = [inverse(r[t] + r_right[t]) for t in tiles]
            ly_left = left(ly, TILES + 1)
            for t in tiles:
                lx = inverse(r[t] + res[i + 1, t, j])
                lz = inverse(r[t] + r_down[t])
                diagonal = ((lx + tx[i - 1, t, j]) + (ly[t] + ly_left[t])) + (lz + above[t])
                inv_diag = jnp.where(r[t] > 2 * NOTHING, inverse(diagonal), 0.0)
                tx[i, t, j], ty[i, t, j], tz[i, t, j] = lx, ly[t], lz
                tyl[i, t, j] = ly_left[t]
                inv[i, t, j] = inv_diag
                update = inv_diag * rem[i, t, j] * (1.0 / middle)
                upd[i, t, j] = update
                if t < TILES:
                    total[i, t, j] = update
                above[t] = lz
            r = r_down
        return carry

    lax.fori_loop(1, WIDE - 1, setup, 0, unroll=2)

    weight_old = 1.0 / sigma
    for sweep in range(1, SWEEPS):
        last = sweep == SWEEPS - 1
        begin, end = 1 + sweep, WIDE - 1 - sweep
        weight_new = 1.0 / (2.0 * sigma - weight_old)
        keep, gain = weight_new * weight_old, 2.0 * weight_new / spread
        weight_old = weight_new
        done = range(TILES) if last else tiles
        src, dst = (upd, res) if sweep % 2 else (res, upd)
        for t in done:
            for j in groups:
                flux[t, j] = tx[begin - 1, t, j] * (src[begin - 1, t, j] - src[begin, t, j])

        def step(i, carry):
            u = [src[i, t, 0] for t in tiles]
            wrap = [next_z(u[t]) for t in done]
            above = [tzu[i, t] * (last_z(src[i, t, GROUPS - 1]) - u[t]) for t in done]
            for j in groups:
                u_down = [src[i, t, j + 1] if j < GROUPS - 1 else (wrap + u)[t] for t in tiles]
                u_right = right(u)
                u_left = left(u, len(done))
                for t in done:
                    fx = tx[i, t, j] * (u[t] - src[i + 1, t, j])
                    fz = tz[i, t, j] * (u[t] - u_down[t])
                    applied = ((fx - flux[t, j]) + (ty[i, t, j] * (u[t] - u_right[t]) + tyl[i, t, j] * (u[t] - u_left[t]))) + (fz - above[t])
                    above[t] = fz
                    flux[t, j] = fx
                    remain = rem[i, t, j] - applied
                    new = keep * u[t] + gain * inv[i, t, j] * remain
                    if last:
                        at = pl.ds(j * STEP + t * CX + i - DEPTH, 8, stride=FAR_ROW)
                        out_ref[at, :] = total[i, t, j] + new
                    else:
                        rem[i, t, j] = remain
                        dst[i, t, j] = new
                        if t < TILES:
                            total[i, t, j] = total[i, t, j] + new
                u = u_down
            return carry

        lax.fori_loop(begin, end, step, 0, unroll=2)


def correct_kernel(gathered_ref, inverse_ref, support_ref, smooth_ref, out_ref, buf, sems):
    zero = jnp.zeros((CF, LANES), jnp.float32)
    sums = [zero] * 4
    order = pair_order(gathered_ref.shape[0] // 2)
    for q in range(gathered_ref.shape[0]):
        row = gathered_ref[pl.ds(2 * order.index(q // 2) + q % 2, 1), :]
        part = inverse_ref[:, q * LANES : (q + 1) * LANES] * row
        sums[q % 4] = sums[q % 4] + part
    total = (sums[0] + sums[1]) + (sums[2] + sums[3])
    column = jnp.broadcast_to(jnp.sum(total, axis=1, keepdims=True), (CF, LANES))
    table = [jnp.broadcast_to(column[c : c + 1, :], (8, LANES)) for c in range(CF)]

    def step(i, carry):
        at = pl.ds(pl.multiple_of(i * 8, 8), 8)
        buf[at, :] = smooth_ref[at, :] + pick(table, support_ref[at, :])
        return carry

    size = ROWS // CHUNKS
    copies = []
    for k in range(CHUNKS):
        lax.fori_loop(k * size // 8, (k + 1) * size // 8, step, 0, unroll=8)
        at = pl.ds(k * size, size)
        copies.append(pltpu.make_async_copy(buf.at[at, :], out_ref.at[at, :], sems.at[k]))
        copies[-1].start()
    for copy in copies:
        copy.wait()


def specs(space, count=1):
    return [pl.BlockSpec(memory_space=space)] * count


def call(kernel, outs, ins, args, out_space=pltpu.VMEM, flops=0, limit=24, **options):
    size = sum(a.size * 4 for a in args) + sum(math.prod(o.shape) * 4 for o in outs)
    return pl.pallas_call(
        kernel,
        out_shape=outs,
        in_specs=ins,
        out_specs=specs(out_space, len(outs)),
        compiler_params=pltpu.CompilerParams(vmem_limit_bytes=limit * 1024 * 1024),
        cost_estimate=pl.CostEstimate(flops=flops, bytes_accessed=size, transcendentals=0),
        **options,
    )(*args)


def held(*shape):
    return pltpu.VMEM(shape, jnp.float32)


def local(residual, classes, class_perm, support, coarse_inverse):
    n_gx, n_gy = lax.axis_size("gx"), lax.axis_size("gy")
    residual, classes, support = rows_of(residual), rows_of(classes), rows_of(support)

    message, own = call(
        coarse_kernel,
        [held(n_gy, STRIP, LANES), held(OWN, LANES)],
        specs(pltpu.HBM, 4),
        [class_perm, residual, support, classes],
        scratch_shapes=[
            pltpu.SMEM(class_perm.shape, jnp.float32),
            pltpu.VMEM((ROWS, LANES), jnp.int32),
            pltpu.VMEM((ROWS, LANES), jnp.int32),
            pltpu.SemaphoreType.DMA,
            pltpu.SemaphoreType.DMA((CHUNKS, 3)),
        ],
        limit=60,
        name="coarse",
    )
    columns = [[turned(k, TURN_Y, n_gy) for k in range(n_gy)]]
    got = lax.all_to_all(message, "gy", 0, 0, axis_index_groups=columns, tiled=True)
    (own,) = call(
        merge_kernel,
        [held(OWN, LANES)],
        specs(pltpu.VMEM, 2),
        [got, own],
        input_output_aliases={1: 0},
        name="merge",
    )
    pairs = [(i, i ^ 1) for i in range(n_gx)]
    others = [step for i in range(1, n_gx - 1, 2) for step in ((i, i + 1), (i + 1, i))]
    mate = lax.ppermute(own, "gx", pairs)
    other = lax.ppermute(own, "gx", others)
    (rows,) = call(
        pair_kernel, [held(n_gx // 2, 2, LANES)], specs(pltpu.VMEM, 2), [own, mate], name="pair"
    )
    groups = [[2 * pair + k for pair in pair_order(n_gx // 2)] for k in range(2)]
    gathered = lax.all_to_all(rows, "gx", 0, 0, axis_index_groups=groups, tiled=True)
    gathered = gathered.reshape(n_gx, LANES)

    planes = pltpu.VMEM((WIDE, TILES + 1, GROUPS, 8, LANES), jnp.float32)
    (smooth,) = call(
        smooth_kernel,
        [held(ROWS, LANES)],
        specs(pltpu.VMEM, 3) + specs(pl.ANY),
        [own, mate, other, rows],
        flops=20_000_000,
        scratch_shapes=[planes] * 8
        + [
            pltpu.VMEM((WIDE, TILES + 1, 8, LANES), jnp.float32),
            pltpu.VMEM((TILES + 1, GROUPS, 8, LANES), jnp.float32),
            pltpu.VMEM((WIDE, TILES, GROUPS, 8, LANES), jnp.float32),
        ],
        name="smooth",
    )
    (out,) = call(
        correct_kernel,
        [jax.ShapeDtypeStruct((ROWS, LANES), jnp.float32)],
        specs(pltpu.VMEM, 4),
        [gathered, coarse_inverse, support, smooth],
        out_space=pltpu.HBM,
        scratch_shapes=[
            pltpu.VMEM((ROWS, LANES), jnp.float32),
            pltpu.SemaphoreType.DMA((CHUNKS,)),
        ],
        name="correct",
    )
    return block_of(out)


def solution(mesh):
    return jax.shard_map(
        local,
        mesh=mesh,
        in_specs=(
            P(None, "gx", "gy"),
            P(None, "gx", "gy"),
            P(),
            P(None, "gx", "gy"),
            P(("gx", "gy"), None),
        ),
        out_specs=P(None, "gx", "gy"),
        check_vma=False,
    )
```
